256 devices in a mesh: col: 64 (over z_hi, y, x, core), row: 4 (over z_lo).
Axes of the slice: x: 4, y: 4, z: 8 (z_hi: 2, z_lo: 4; z = z_hi * 4 + z_lo), core: 2. Of those that a mesh axis runs over, the one named last changes fastest.
Arguments:
- greens_matrix: float32 [16384, 16384], P('col', 'row'), may hold values from -6 to 6
- dest_ids: int32 [16384], P('col'), may hold values from 0 to 16383, as said below
- send_slot: int32 [64], P('col'), may hold values from 0 to 1
Outputs:
- rotated: float32 [16384, 16384], P('col', 'row')
The draws below stay inside these ranges and needn't reach their ends.
Inputs may be any that keep to these rules, and one draw needn't show every extreme that they name: `dest_ids`: every value occurs once. Value v belongs to the device v // 256 of col. The sources that one device holds go to at most 8 of any one device's values, and every device sends exactly 8 to one device and receives exactly 8 from one device. The number that device s sends to device (s + o) mod 64 depends on o only.
All inputs are finite; a program needn't handle non-finite values.
Results may differ from the reference program's by a relative error of at most 0.00055.
Values sent between devices are 32-bit elements; how exact they have to be, the bound alone decides.
A program may use at most 128 MiB of HBM per device.

```python
import jax
import jax.numpy as jnp
from jax import lax

B = 128
SWEEPS = 2
N = 16384
M = 16384
CAP = 8
N_COL = 64


def draw_dest_ids(key, part):
    pair_cols = 2 * B
    slot_count = N_COL * CAP
    key_pin, key_score, key_perm = jax.random.split(jax.random.fold_in(key, 17), 3)
    pinned = jax.random.randint(key_pin, (), 0, N_COL)
    slot_offset = jnp.arange(slot_count, dtype=jnp.int32) // CAP
    scores = jax.random.randint(key_score, (slot_count,), 0, 1 << 20) * slot_count + jnp.arange(slot_count, dtype=jnp.int32)
    scores = jnp.where(slot_offset == pinned, scores + (1 << 30), scores)
    top_scores, chosen = jax.lax.top_k(scores, pair_cols)
    offsets = slot_offset[chosen]
    counts = jnp.sum((offsets[:, None] == jnp.arange(N_COL, dtype=jnp.int32)[None, :]).astype(jnp.int32), axis=0)
    base = jnp.cumsum(counts) - counts

    def sender_ids(sender):
        order = jax.random.permutation(jax.random.fold_in(key_perm, sender), pair_cols)
        local_offset = offsets[order]
        same_offset = local_offset[:, None] == local_offset[None, :]
        earlier = jnp.arange(pair_cols)[None, :] < jnp.arange(pair_cols)[:, None]
        rank_local = jnp.sum((same_offset & earlier).astype(jnp.int32), axis=1)
        target_dev = (sender + local_offset) % N_COL
        return (target_dev * pair_cols + base[local_offset] + rank_local).astype(jnp.int32)
    every_id = jax.vmap(sender_ids)(jnp.arange(N_COL, dtype=jnp.int32))
    return every_id.reshape(-1).astype(jnp.int32)


def with_ends(result, rng, smallest, largest):
    longest = result.shape.index(max(result.shape))
    spots = []
    for shift in (0, 1):
        where = [jax.random.randint(jax.random.fold_in(rng, axis), (), 0, length) for axis, length in enumerate(result.shape)]
        where[longest] = (where[longest] + shift) % result.shape[longest]
        spots.append(tuple(where))
    return result.at[spots[0]].set(smallest).at[spots[1]].set(largest)


def block_levels(key, extent, pieces, low, high):
    def one(position, parts):
        draws = jax.random.uniform(jax.random.fold_in(jax.random.fold_in(key, 6), position), (parts,), jnp.float32, low / len(pieces), high / len(pieces))
        return jnp.repeat(jnp.exp(draws), extent[position] // parts).reshape((-1,) + (1,) * (len(extent) - position - 1))

    level = one(*pieces[0])
    for cut in pieces[1:]:
        level = level * one(*cut)
    return level


def centred(key, shape, spread, bound, cuts=(), held_as=jnp.bfloat16):
    array = spread * jax.random.normal(key, shape, jnp.float32)
    if cuts:
        array = array * block_levels(key, shape, cuts, -0.22, 0.18)
    return jnp.clip(array, -bound, bound).astype(held_as)


def setup_inputs(seed: int = 0) -> dict:
    arg_keys = jax.random.split(jax.random.key(seed), 4)
    greens_matrix = centred(arg_keys[0], (N, M), 1.0, 6.0, ((0, 64), (1, 4)), jnp.float32)
    dest_ids = draw_dest_ids(jax.random.fold_in(arg_keys[3], 71), 0)
    send_slot = with_ends(jax.random.randint(arg_keys[2], (N_COL,), 0, 2), jax.random.fold_in(arg_keys[2], 1), 0, 1).astype(jnp.int32)
    return {"greens_matrix": greens_matrix, "dest_ids": dest_ids, "send_slot": send_slot}


def orthogonal_steps(pair_gram):
    size = pair_gram.shape[0]
    rotation = jnp.eye(size, dtype=jnp.float32)
    for sweep_index in range(SWEEPS):
        squared = jnp.dot(pair_gram, pair_gram, precision=lax.Precision.HIGHEST)
        factor = jnp.linalg.cholesky(squared)
        q_transposed = jax.scipy.linalg.solve_triangular(factor, pair_gram, lower=True)
        left_side = jnp.dot(q_transposed, pair_gram, precision=lax.Precision.HIGHEST)
        rotated_gram = jnp.dot(left_side, q_transposed.T, precision=lax.Precision.HIGHEST)
        pair_gram = 0.5 * (rotated_gram + rotated_gram.T)
        rotation = jnp.dot(rotation, q_transposed.T, precision=lax.Precision.HIGHEST)
    return rotation

def solve_pair(columns_block):
    pair_gram = jnp.dot(columns_block, columns_block.T, precision=lax.Precision.HIGHEST)
    rotation = orthogonal_steps(pair_gram)
    return jnp.dot(rotation.T, columns_block, precision=lax.Precision.HIGHEST)

def reference(greens_matrix, dest_ids, send_slot):
    placed = jnp.zeros_like(greens_matrix).at[dest_ids].set(greens_matrix)
    pair_blocks = placed.reshape(N_COL, 2 * B, M)
    turned = lax.map(solve_pair, pair_blocks)
    halves = turned.reshape(N_COL, 2, B, M)
    first_out = (send_slot == 0)[:, None, None]
    outbound = jnp.where(first_out, halves[:, 0], halves[:, 1])
    retained = jnp.where(first_out, halves[:, 1], halves[:, 0])
    received = jnp.roll(outbound, N_COL // 2, axis=0)
    paired = jnp.concatenate([retained, received], axis=1)
    final_blocks = lax.map(solve_pair, paired)
    return final_blocks.reshape(N, M)
```

```python
import functools

import jax
import jax.numpy as jnp
from jax import lax
from jax.experimental import pallas as pl
from jax.experimental.pallas import tpu as pltpu
from jax.sharding import PartitionSpec as P

CHUNKS = 8
BLOCK = 64
F32 = jnp.float32
BF16 = jnp.bfloat16
MESH = pl.DeviceIdType.MESH
HIGHEST = lax.Precision.HIGHEST


def split3(value):
    high = value.astype(BF16)
    rest = value - high.astype(F32)
    middle = rest.astype(BF16)
    low = (rest - middle.astype(F32)).astype(BF16)
    return high, middle, low


def select_rows(one_hot, value):
    high, middle, low = split3(value)
    dot = functools.partial(jnp.dot, one_hot, preferred_element_type=F32)
    return (dot(high) + dot(middle)) + dot(low)


def dot_f32(a, b, dims=((1,), (0,))):
    return lax.dot_general(a, b, (dims, ((), ())), precision=HIGHEST, preferred_element_type=F32)


def gram_update(rows):
    high, middle, low = split3(rows)
    nt = (((1,), (1,)), ((), ()))
    dot = functools.partial(lax.dot_general, dimension_numbers=nt, preferred_element_type=F32)
    cross = dot(middle, high) + dot(low, high)
    return dot(high, high) + dot(middle, middle) + cross, cross


def exchange_kernel(
    peers, x_ref, slot_source_ref, row_slot_ref,
    own_hbm, other_hbm, both_hbm, tri_ref,
    out_buf, in_buf, both_buf, other_buf, gram_buf, cross_buf,
    out_sem, in_sem, z_out_sem, z_in_sem, write_sem,
):
    col = lax.axis_index("col")
    side = col // peers
    me = col % peers
    mirror = lax.rem(col + peers, 2 * peers)
    half = CHUNKS // 2
    slots = out_buf.shape[2]
    width = out_buf.shape[3]
    rows = other_buf.shape[1]

    barrier = pltpu.get_barrier_semaphore()

    def greet(step, carry):
        peer = side * peers + lax.rem(me + step, peers)
        pl.semaphore_signal(barrier, inc=1, device_id={"col": peer}, device_id_type=MESH)
        return carry

    lax.fori_loop(1, peers, greet, 0)
    pl.semaphore_signal(barrier, inc=1, device_id={"col": mirror}, device_id_type=MESH)
    pl.semaphore_wait(barrier, peers)

    place = lax.broadcasted_iota(jnp.int32, (peers * slots, rows), 1)
    pack = (slot_source_ref[...] == place).astype(BF16)

    def send_chunk(index, carry):
        chunk = lax.rem((1 - side) * half + index, CHUNKS)
        piece = x_ref[:, pl.ds(pl.multiple_of(chunk * width, width), width)]
        packed = select_rows(pack, piece).reshape(peers, slots, width)
        out_buf[index] = packed

        def send(step, inner):
            peer = lax.rem(me + step, peers)
            pltpu.make_async_remote_copy(
                src_ref=out_buf.at[index, peer],
                dst_ref=in_buf.at[index, me],
                send_sem=out_sem.at[index],
                recv_sem=in_sem.at[index],
                device_id={"col": side * peers + peer},
                device_id_type=MESH,
            ).start()
            return inner

        lax.fori_loop(1, peers, send, 0)
        in_buf[index, me] = out_buf[index, me]
        return carry

    lax.fori_loop(0, CHUNKS, send_chunk, 0)

    slot = lax.broadcasted_iota(jnp.int32, (rows, peers * slots), 1)
    compact = (row_slot_ref[...] == slot).astype(BF16)

    def arrived(index):
        pltpu.make_async_copy(
            in_buf.at[index, pl.ds(0, peers - 1)], in_buf.at[index, pl.ds(0, peers - 1)], in_sem.at[index]
        ).wait()
        return select_rows(compact, in_buf[index].reshape(peers * slots, width))

    def cross_copy(index):
        return pltpu.make_async_remote_copy(
            src_ref=other_buf.at[index],
            dst_ref=both_buf.at[index, pl.ds(pl.multiple_of(side * rows, rows), rows)],
            send_sem=z_out_sem.at[index],
            recv_sem=z_in_sem.at[index],
            device_id={"col": mirror},
            device_id_type=MESH,
        )

    def write_other(index):
        return pltpu.make_async_copy(other_buf.at[index], other_hbm.at[index], write_sem.at[index])

    def write_own(index):
        source = both_buf.at[index, pl.ds(pl.multiple_of(side * rows, rows), rows)]
        return pltpu.make_async_copy(source, own_hbm.at[index], write_sem.at[half + index])

    def write_both(index):
        return pltpu.make_async_copy(both_buf.at[index], both_hbm.at[index], write_sem.at[2 * half + index])

    def cross_chunk(index, carry):
        other_buf[index] = arrived(index)
        cross_copy(index).start()
        write_other(index).start()
        return carry

    lax.fori_loop(0, half, cross_chunk, 0)

    def keep_chunk(index, carry):
        both_buf[index, pl.ds(pl.multiple_of(side * rows, rows), rows)] = arrived(half + index)
        write_own(index).start()
        return carry

    lax.fori_loop(0, half, keep_chunk, 0)

    gram_buf[...] = jnp.zeros_like(gram_buf)
    cross_buf[...] = jnp.zeros_like(cross_buf)

    def gram_chunk(index, carry):
        cross_copy(index).wait_recv()
        write_both(index).start()
        total, cross = gram_update(both_buf[index])
        gram_buf[...] += total
        cross_buf[...] += cross
        return carry

    lax.fori_loop(0, half, gram_chunk, 0)
    gram = gram_buf[...] + cross_buf[...].T
    quarter = rows // 2
    place = 0
    for i in range(4):
        for j in range(i + 1):
            tri_ref[place * quarter:(place + 1) * quarter, :] = gram[
                i * quarter:(i + 1) * quarter, j * quarter:(j + 1) * quarter
            ]
            place += 1

    def finish(index, carry):
        cross_copy(index).wait_send()
        write_other(index).wait()
        write_own(index).wait()
        write_both(index).wait()
        return carry

    lax.fori_loop(0, half, finish, 0)

    def sent(index, carry):
        pltpu.make_async_copy(
            out_buf.at[index, pl.ds(0, peers - 1)], out_buf.at[index, pl.ds(0, peers - 1)], out_sem.at[index]
        ).wait()
        return carry

    lax.fori_loop(0, CHUNKS, sent, 0)


def exchange(x, slot_source, row_slot, peers):
    rows, columns = x.shape
    width = columns // CHUNKS
    half = CHUNKS // 2
    slots = slot_source.shape[0] // peers
    any_space = pl.BlockSpec(memory_space=pl.ANY)
    vmem = pl.BlockSpec(memory_space=pltpu.VMEM)
    return pl.pallas_call(
        functools.partial(exchange_kernel, peers),
        out_shape=[
            jax.ShapeDtypeStruct((half, rows, width), F32),
            jax.ShapeDtypeStruct((half, rows, width), F32),
            jax.ShapeDtypeStruct((half, 2 * rows, width), F32),
            jax.ShapeDtypeStruct((10 * rows // 2, rows // 2), F32),
        ],
        in_specs=[vmem, vmem, vmem],
        out_specs=[any_space, any_space, any_space, vmem],
        scratch_shapes=[
            pltpu.VMEM((CHUNKS, peers, slots, width), F32),
            pltpu.VMEM((CHUNKS, peers, slots, width), F32),
            pltpu.VMEM((half, 2 * rows, width), F32),
            pltpu.VMEM((half, rows, width), F32),
            pltpu.VMEM((2 * rows, 2 * rows), F32),
            pltpu.VMEM((2 * rows, 2 * rows), F32),
            pltpu.SemaphoreType.DMA((CHUNKS,)),
            pltpu.SemaphoreType.DMA((CHUNKS,)),
            pltpu.SemaphoreType.DMA((half,)),
            pltpu.SemaphoreType.DMA((half,)),
            pltpu.SemaphoreType.DMA((3 * half,)),
        ],
        compiler_params=pltpu.CompilerParams(
            collective_id=0, has_side_effects=True, vmem_limit_bytes=56 << 20
        ),
        cost_estimate=pl.CostEstimate(flops=10**10, bytes_accessed=10**8, transcendentals=0),
        name="exchange",
    )(x, slot_source, row_slot)


def sum_kernel(peers, row_count, tri_ref, out_ref, parts, total, out_sem, in_sem, back_out_sem, back_in_sem):
    col = lax.axis_index("col")
    side = col // peers
    row = lax.axis_index("row")
    count = 2 * row_count
    me = side * row_count + row
    size = parts.shape[1]

    def device(index):
        return {"col": (index // row_count) * peers + col % peers, "row": index % row_count}

    barrier = pltpu.get_barrier_semaphore()
    for step in range(1, count):
        pl.semaphore_signal(barrier, inc=1, device_id=device(lax.rem(me + step, count)), device_id_type=MESH)
    pl.semaphore_wait(barrier, count - 1)

    def piece(index):
        return pl.ds(pl.multiple_of(index * size, size), size)

    for step in range(1, count):
        to = lax.rem(me + step, count)
        pltpu.make_async_remote_copy(
            src_ref=tri_ref.at[piece(to)], dst_ref=parts.at[me], send_sem=out_sem, recv_sem=in_sem,
            device_id=device(to), device_id_type=MESH,
        ).start()
    parts[me] = tri_ref[piece(me), :]
    several = parts.at[pl.ds(0, count - 1)]
    pltpu.make_async_copy(several, several, in_sem).wait()
    value = parts[0]
    for index in range(1, count):
        value = value + parts[index]
    total[me] = value
    for step in range(1, count):
        to = lax.rem(me + step, count)
        pltpu.make_async_remote_copy(
            src_ref=total.at[me], dst_ref=total.at[me], send_sem=back_out_sem, recv_sem=back_in_sem,
            device_id=device(to), device_id_type=MESH,
        ).start()
    several = total.at[pl.ds(0, count - 1)]
    pltpu.make_async_copy(several, several, back_in_sem).wait()
    out_ref[...] = total[...].reshape(out_ref.shape)
    pltpu.make_async_copy(several, several, out_sem).wait()
    pltpu.make_async_copy(several, several, back_out_sem).wait()


def sum_over_devices(tri, peers, row_count):
    count = 2 * row_count
    size = tri.shape[0] // count
    vmem = pl.BlockSpec(memory_space=pltpu.VMEM)
    return pl.pallas_call(
        functools.partial(sum_kernel, peers, row_count),
        out_shape=jax.ShapeDtypeStruct(tri.shape, F32),
        in_specs=[vmem],
        out_specs=vmem,
        scratch_shapes=[
            pltpu.VMEM((count, size, tri.shape[1]), F32),
            pltpu.VMEM((count, size, tri.shape[1]), F32),
            pltpu.SemaphoreType.DMA,
            pltpu.SemaphoreType.DMA,
            pltpu.SemaphoreType.DMA,
            pltpu.SemaphoreType.DMA,
        ],
        compiler_params=pltpu.CompilerParams(collective_id=1, has_side_effects=True),
        cost_estimate=pl.CostEstimate(flops=10**9, bytes_accessed=10**8, transcendentals=0),
        name="sum_over_devices",
    )(tri)


def inverse_factors(blocks):
    size = BLOCK
    groups = size // 8
    sublane = lax.broadcasted_iota(jnp.int32, (8, 2 * size), 0)
    lane = lax.broadcasted_iota(jnp.int32, (8, 2 * size), 1)
    held = []
    for block in blocks:
        parts = []
        for g in range(groups):
            unit = (lane == sublane + (size + 8 * g)).astype(F32)
            left = jnp.concatenate([block[8 * g:8 * g + 8, :], jnp.zeros((8, size), F32)], axis=1)
            parts.append(left + unit)
        held.append(parts)
    for j in range(size):
        first, within = divmod(j, 8)
        for parts in held:
            row = parts[first][within:within + 1, :]
            scaled = row * (1.0 / row[:, j:j + 1])
            for g in range(first, groups):
                column = parts[g][:, j:j + 1]
                if g == first:
                    column = jnp.where(sublane[:, :1] > within, column, 0.0)
                parts[g] = parts[g] - column * scaled
    result = []
    for parts in held:
        rows = []
        for g in range(groups):
            pivot = jnp.sum(jnp.where(lane == sublane + 8 * g, parts[g], 0.0), axis=1, keepdims=True)
            rows.append(parts[g] * lax.rsqrt(pivot))
        result.append(jnp.concatenate(rows, axis=0)[:, size:])
    return result


def eliminate(work_refs, width):
    size = work_refs[0].shape[0]
    for start in range(0, size, BLOCK):
        stop = start + BLOCK
        inverses = inverse_factors([work[start:stop, start:stop] for work in work_refs])
        base = start - start % 128
        for work, inverse in zip(work_refs, inverses):
            top = dot_f32(inverse, work[start:stop, base:width])
            work[start:stop, base:width] = top
            if stop < size:
                below = top[:, stop - base:size - base]
                work[stop:size, base:width] = work[stop:size, base:width] - dot_f32(below, top, ((0,), (0,)))


def orthogonal_steps(grams, work_refs):
    size = grams[0].shape[0]
    row = lax.broadcasted_iota(jnp.int32, (size, size), 0)
    column = lax.broadcasted_iota(jnp.int32, (size, size), 1)
    for gram, work in zip(grams, work_refs):
        trace = jnp.sum(jnp.where(row == column, gram, 0.0))
        gram = gram * (size / trace)
        work[:, :size] = dot_f32(gram, gram)
    eliminate(work_refs, size)
    for work in work_refs:
        factor = jnp.where(row <= column, work[:, :size], 0.0)
        work[:, :size] = dot_f32(factor, factor, ((1,), (1,)))
        work[:, size:] = factor
    eliminate(work_refs, 2 * size)
    return [work[:, size:] for work in work_refs]


def rotation_kernel(tri_ref, position_ref, own_slot_ref, partner_slot_ref, weight_ref, gram_buf, work_a, work_b):
    quarter = tri_ref.shape[1]
    size = 2 * quarter
    place = 0
    for i in range(4):
        for j in range(i + 1):
            block = tri_ref[place * quarter:(place + 1) * quarter, :]
            gram_buf[i * quarter:(i + 1) * quarter, j * quarter:(j + 1) * quarter] = block
            if i != j:
                gram_buf[j * quarter:(j + 1) * quarter, i * quarter:(i + 1) * quarter] = block.T
            place += 1
    slot = lax.broadcasted_iota(jnp.int32, (2 * size, 2 * size), 0)
    place_of = (slot == position_ref[...]).astype(BF16)
    half_way = select_rows(place_of, gram_buf[...])
    gram_buf[...] = select_rows(place_of, half_way.T)
    own = gram_buf[:size, :size]
    partner = gram_buf[size:, size:]
    between = gram_buf[:size, size:]
    own_turn, partner_turn = orthogonal_steps([own, partner], [work_a, work_b])
    own_part = jnp.where(own_slot_ref[0] == 0, own_turn[quarter:], own_turn[:quarter])
    partner_part = jnp.where(partner_slot_ref[0] == 0, partner_turn[:quarter], partner_turn[quarter:])
    nt = ((1,), (1,))
    upper = dot_f32(dot_f32(own_part, own), own_part, nt)
    lower = dot_f32(dot_f32(partner_part, partner), partner_part, nt)
    mixed = dot_f32(dot_f32(own_part, between), partner_part, nt)
    gram_buf[:quarter, :quarter] = upper
    gram_buf[quarter:size, quarter:size] = lower
    gram_buf[:quarter, quarter:size] = mixed
    gram_buf[quarter:size, :quarter] = mixed.T
    second = gram_buf[:size, :size]
    (last,) = orthogonal_steps([0.5 * (second + second.T)], [work_a])
    gram_buf[:size, :size] = dot_f32(last[:, :quarter], own_part)
    gram_buf[:size, size:] = dot_f32(last[:, quarter:], partner_part)
    high, middle, low = split3(gram_buf[:size, :])
    dot = functools.partial(jnp.dot, preferred_element_type=F32)
    weight_ref[...] = (dot(high, place_of) + dot(middle, place_of)) + dot(low, place_of)


def rotations(tri, position, own_slot, partner_slot):
    size = 2 * tri.shape[1]
    vmem = pl.BlockSpec(memory_space=pltpu.VMEM)
    smem = pl.BlockSpec(memory_space=pltpu.SMEM)
    return pl.pallas_call(
        rotation_kernel,
        out_shape=jax.ShapeDtypeStruct((size, 2 * size), F32),
        in_specs=[vmem, vmem, smem, smem],
        out_specs=vmem,
        scratch_shapes=[
            pltpu.VMEM((2 * size, 2 * size), F32),
            pltpu.VMEM((size, 2 * size), F32),
            pltpu.VMEM((size, 2 * size), F32),
        ],
        compiler_params=pltpu.CompilerParams(vmem_limit_bytes=32 << 20),
        cost_estimate=pl.CostEstimate(flops=6 * 10**10, bytes_accessed=10**8, transcendentals=0),
        name="rotations",
    )(tri, position, own_slot, partner_slot)


def product3(a, b):
    a_high = a.astype(BF16)
    a_low = (a - a_high.astype(F32)).astype(BF16)
    b_high = b.astype(BF16)
    b_low = (b - b_high.astype(F32)).astype(BF16)
    dot = functools.partial(jnp.dot, preferred_element_type=F32)
    return dot(a_high, b_high) + (dot(a_high, b_low) + dot(a_low, b_high))


def apply_both_kernel(start_ref, weight_ref, both_ref, out_ref):
    out_ref[...] = product3(weight_ref[...], both_ref[0])


def apply_both(start, weight, both, columns):
    chunks, rows, width = both.shape
    size = weight.shape[0]
    return pl.pallas_call(
        apply_both_kernel,
        grid_spec=pltpu.PrefetchScalarGridSpec(
            num_scalar_prefetch=1,
            grid=(chunks,),
            in_specs=[
                pl.BlockSpec((size, rows), lambda i, s: (0, 0)),
                pl.BlockSpec((1, rows, width), lambda i, s: (i, 0, 0)),
            ],
            out_specs=pl.BlockSpec((size, width), lambda i, s: (0, s[0] * chunks + i)),
        ),
        out_shape=jax.ShapeDtypeStruct((size, columns), F32),
        cost_estimate=pl.CostEstimate(flops=10**10, bytes_accessed=10**7, transcendentals=0),
        compiler_params=pltpu.CompilerParams(vmem_limit_bytes=32 << 20),
        name="apply_both",
    )(start, weight, both)


def apply_rest_kernel(start_ref, weight_ref, own_ref, mirror_ref, partial_ref, out_ref):
    rows = own_ref.shape[1]
    side = start_ref[0]
    own_weight = jnp.where(side == 0, weight_ref[:, :rows], weight_ref[:, rows:])
    mirror_weight = jnp.where(side == 0, weight_ref[:, rows:], weight_ref[:, :rows])
    out_ref[...] = product3(own_weight, own_ref[0]) + product3(mirror_weight, mirror_ref[0])


def apply_rest(start, weight, own, mirror, partial):
    chunks, rows, width = own.shape
    size = weight.shape[0]
    return pl.pallas_call(
        apply_rest_kernel,
        grid_spec=pltpu.PrefetchScalarGridSpec(
            num_scalar_prefetch=1,
            grid=(chunks,),
            in_specs=[
                pl.BlockSpec((size, 2 * rows), lambda i, s: (0, 0)),
                pl.BlockSpec((1, rows, width), lambda i, s: (i, 0, 0)),
                pl.BlockSpec((1, rows, width), lambda i, s: (i, 0, 0)),
                pl.BlockSpec(memory_space=pl.ANY),
            ],
            out_specs=pl.BlockSpec((size, width), lambda i, s: (0, (1 - s[0]) * chunks + i)),
        ),
        out_shape=jax.ShapeDtypeStruct(partial.shape, F32),
        input_output_aliases={4: 0},
        cost_estimate=pl.CostEstimate(flops=10**10, bytes_accessed=10**7, transcendentals=0),
        compiler_params=pltpu.CompilerParams(vmem_limit_bytes=32 << 20),
        name="apply_rest",
    )(start, weight, own, mirror, partial)


def slot_tables(dest_ids, col, peers, slots):
    rows = dest_ids.shape[0]
    count = 2 * peers
    local = jnp.arange(rows, dtype=jnp.int32)
    target = dest_ids // rows
    peer = target % peers
    earlier = (peer[:, None] == peer[None, :]) & (local[None, :] < local[:, None])
    rank = jnp.sum(earlier.astype(jnp.int32), axis=1)
    wanted = jnp.arange(peers * slots, dtype=jnp.int32)
    slot = peer * slots + rank
    slot_source = jnp.max(jnp.where(slot[None, :] == wanted[:, None], local[None, :], -1), axis=1)
    offset = (target - col) % peers
    amount = jnp.sum((offset[None, :] == jnp.arange(peers, dtype=jnp.int32)[:, None]).astype(jnp.int32), axis=1)
    sender = jnp.arange(peers, dtype=jnp.int32)
    sender_offset = (col - sender) % peers
    from_sender = jnp.sum(
        jnp.where(sender_offset[:, None] == jnp.arange(peers, dtype=jnp.int32)[None, :], amount[None, :], 0), axis=1
    )
    base = jnp.sum(jnp.where(sender[None, :] < sender[:, None], from_sender[None, :], 0), axis=1)
    within = jnp.arange(slots, dtype=jnp.int32)
    row_of_slot = jnp.where(within[None, :] < from_sender[:, None], base[:, None] + within[None, :], -1).reshape(-1)
    row_slot = jnp.max(jnp.where(row_of_slot[None, :] == local[:, None], wanted[None, :], -1), axis=1)
    return slot_source[:, None], row_slot[:, None]


def final_positions(every_id, col, peers, slots):
    devices, rows = every_id.shape
    target = every_id // rows
    mine = target % peers == col % peers
    place = jnp.where(target == col, 0, rows) + every_id % rows
    local = jnp.arange(rows, dtype=jnp.int32)
    before = (local[:, None] < local[None, :]).astype(BF16)
    rank = jnp.dot(mine.astype(BF16), before, preferred_element_type=F32).astype(jnp.int32)
    within = jnp.arange(slots, dtype=jnp.int32)
    held = jnp.max(
        jnp.where(mine[:, None, :] & (rank[:, None, :] == within[None, :, None]), place[:, None, :], -1), axis=2
    )
    amount = jnp.sum(mine.astype(jnp.int32), axis=1)
    device = jnp.arange(devices, dtype=jnp.int32)
    base = jnp.sum(jnp.where(device[None, :] < device[:, None], amount[None, :], 0), axis=1)
    row_of = jnp.where(held >= 0, base[:, None] + within[None, :], -1).reshape(-1)
    wanted = jnp.arange(2 * rows, dtype=jnp.int32)
    position = jnp.max(jnp.where(row_of[:, None] == wanted[None, :], held.reshape(-1)[:, None], -1), axis=0)
    return position[None, :]


def body(row_count, greens_matrix, dest_ids, send_slot):
    rows, columns = greens_matrix.shape
    count = lax.axis_size("col")
    peers = count // 2
    cap = max(2, 2 * rows // count)
    slots = 2 * cap
    col = lax.axis_index("col")
    every_id = lax.all_gather(dest_ids, "col")
    every_slot = lax.all_gather(send_slot, "col").reshape(-1)
    slot_source, row_slot = slot_tables(dest_ids, col, peers, slots)
    own, other, both, tri = exchange(greens_matrix, slot_source, row_slot, peers)
    mirror = lax.ppermute(own, "col", [(i, i ^ peers) for i in range(count)])
    tri = sum_over_devices(tri, peers, row_count)
    position = final_positions(every_id, col, peers, slots)
    device = jnp.arange(count, dtype=jnp.int32)
    partner_slot = jnp.sum(jnp.where(device == (col + peers) % count, every_slot, 0))[None]
    weight = rotations(tri, position, send_slot, partner_slot)
    side = (col // peers).astype(jnp.int32)[None]
    partial = apply_both(side, weight, both, columns)
    return apply_rest(side, weight, other, mirror, partial)


def solution(mesh):
    return jax.shard_map(
        functools.partial(body, mesh.shape["row"]),
        mesh=mesh,
        in_specs=(P("col", "row"), P("col"), P("col")),
        out_specs=P("col", "row"),
        check_vma=False,
    )
```

```python
import functools

import jax
import jax.numpy as jnp
from jax import lax
from jax.experimental import pallas as pl
from jax.experimental.pallas import tpu as pltpu
from jax.sharding import PartitionSpec as P

CHUNKS = 16
EARLY = 3
BLOCK = 64
F32 = jnp.float32
BF16 = jnp.bfloat16
MESH = pl.DeviceIdType.MESH
HIGHEST = lax.Precision.HIGHEST


def split3(value):
    high = value.astype(BF16)
    rest = value - high.astype(F32)
    middle = rest.astype(BF16)
    low = (rest - middle.astype(F32)).astype(BF16)
    return high, middle, low


def select_rows(one_hot, value):
    high, middle, low = split3(value)
    dot = functools.partial(jnp.dot, one_hot, preferred_element_type=F32)
    return (dot(high) + dot(middle)) + dot(low)


def dot_f32(a, b, dims=((1,), (0,))):
    return lax.dot_general(a, b, (dims, ((), ())), precision=HIGHEST, preferred_element_type=F32)


def gram_update(rows):
    high, middle, low = split3(rows)
    nt = (((1,), (1,)), ((), ()))
    dot = functools.partial(lax.dot_general, dimension_numbers=nt, preferred_element_type=F32)
    cross = dot(middle, high) + dot(low, high)
    return dot(high, high) + dot(middle, middle) + cross, cross


def exchange_kernel(
    peers, row_count, x_ref, slot_source_ref, slot_place_ref, row_slot_ref, send_slot_ref,
    own_hbm, other_hbm, both_hbm, early_hbm, tri_ref, note_ref,
    out_buf, in_buf, both_buf, other_buf, early_buf, gram_buf, cross_buf, place_out, place_in, note_out, note_in,
    tri_buf, parts, total,
    out_sem, in_sem, z_out_sem, z_in_sem, write_sem, place_sem, note_sem, early_sem, sum_sem,
):
    col = lax.axis_index("col")
    side = col // peers
    me = col % peers
    mirror = lax.rem(col + peers, 2 * peers)
    half = CHUNKS // 2
    slots = out_buf.shape[2]
    width = out_buf.shape[3]
    rows = other_buf.shape[1]

    barrier = pltpu.get_barrier_semaphore()

    def greet(step, carry):
        peer = side * peers + lax.rem(me + step, peers)
        pl.semaphore_signal(barrier, inc=1, device_id={"col": peer}, device_id_type=MESH)
        return carry

    count = 2 * row_count
    ring = side * row_count + lax.axis_index("row")

    def ring_device(step):
        index = lax.rem(ring + step, count)
        return {"col": (index // row_count) * peers + me, "row": index % row_count}

    lax.fori_loop(1, peers, greet, 0)
    for step in range(1, count):
        pl.semaphore_signal(barrier, inc=1, device_id=ring_device(step), device_id_type=MESH)
    pl.semaphore_wait(barrier, peers - 1 + count - 1)

    place = lax.broadcasted_iota(jnp.int32, (rows, peers * slots), 0)
    pack = (slot_source_ref[...] == place).astype(F32).T.astype(BF16)

    def send_chunk(index, carry):
        chunk = lax.rem((1 - side) * half + index, CHUNKS)
        piece = x_ref[:, pl.ds(pl.multiple_of(chunk * width, width), width)]
        packed = select_rows(pack, piece).reshape(peers, slots, width)
        out_buf[index] = packed

        def send(step, inner):
            peer = lax.rem(me + step, peers)
            pltpu.make_async_remote_copy(
                src_ref=out_buf.at[index, peer],
                dst_ref=in_buf.at[index, me],
                send_sem=out_sem.at[index],
                recv_sem=in_sem.at[index],
                device_id={"col": side * peers + peer},
                device_id_type=MESH,
            ).start()
            return inner

        lax.fori_loop(1, peers, send, 0)
        in_buf[index, me] = out_buf[index, me]
        return carry

    lax.fori_loop(0, CHUNKS, send_chunk, 0)

    places = jnp.broadcast_to(slot_place_ref[...].astype(F32), (128, peers * slots)).T
    place_out[...] = places.reshape(peers, slots, 128)

    def send_places(step, carry):
        peer = lax.rem(me + step, peers)
        pltpu.make_async_remote_copy(
            src_ref=place_out.at[peer],
            dst_ref=place_in.at[me],
            send_sem=place_sem.at[0],
            recv_sem=place_sem.at[1],
            device_id={"col": side * peers + peer},
            device_id_type=MESH,
        ).start()
        return carry

    lax.fori_loop(1, peers, send_places, 0)
    place_in[me] = place_out[me]

    slot = lax.broadcasted_iota(jnp.int32, (peers * slots, rows), 0)
    compact = (row_slot_ref[...] == slot).astype(F32).T.astype(BF16)

    def arrived(index):
        pltpu.make_async_copy(
            in_buf.at[index, pl.ds(0, peers - 1)], in_buf.at[index, pl.ds(0, peers - 1)], in_sem.at[index]
        ).wait()
        return select_rows(compact, in_buf[index].reshape(peers * slots, width))

    def cross_copy(index):
        return pltpu.make_async_remote_copy(
            src_ref=other_buf.at[index],
            dst_ref=both_buf.at[index, pl.ds(pl.multiple_of(side * rows, rows), rows)],
            send_sem=z_out_sem.at[index],
            recv_sem=z_in_sem.at[index],
            device_id={"col": mirror},
            device_id_type=MESH,
        )

    def write_other(index):
        return pltpu.make_async_copy(other_buf.at[index], other_hbm.at[index], write_sem.at[index])

    def write_own(index):
        source = both_buf.at[EARLY + index, pl.ds(pl.multiple_of(side * rows, rows), rows)]
        return pltpu.make_async_copy(source, own_hbm.at[index], write_sem.at[half + index])

    def write_both(index):
        return pltpu.make_async_copy(both_buf.at[index], both_hbm.at[index], write_sem.at[2 * half + index])

    def cross_chunk(index, carry):
        other_buf[index] = arrived(index)
        cross_copy(index).start()
        write_other(index).start()
        return carry

    lax.fori_loop(0, half, cross_chunk, 0)

    def keep_chunk(index, carry):
        both_buf[index, pl.ds(pl.multiple_of(side * rows, rows), rows)] = arrived(half + index)
        return carry

    lax.fori_loop(0, half, keep_chunk, 0)
    for index in range(half - EARLY):
        write_own(index).start()

    several = place_in.at[pl.ds(0, peers - 1)]
    pltpu.make_async_copy(several, several, place_sem.at[1]).wait()
    listed = select_rows(compact, place_in[...].reshape(peers * slots, 128)).T[:8]
    first_row = lax.broadcasted_iota(jnp.int32, listed.shape, 0) == 0
    note_out[...] = jnp.where(first_row, listed, send_slot_ref[0].astype(F32))
    note_in[side] = note_out[...]
    note_copy = pltpu.make_async_remote_copy(
        src_ref=note_out,
        dst_ref=note_in.at[side],
        send_sem=note_sem.at[0],
        recv_sem=note_sem.at[1],
        device_id={"col": mirror},
        device_id_type=MESH,
    )
    note_copy.start()

    gram_buf[...] = jnp.zeros_like(gram_buf)
    cross_buf[...] = jnp.zeros_like(cross_buf)

    def early_copy(index):
        return pltpu.make_async_remote_copy(
            src_ref=both_buf.at[index, pl.ds(pl.multiple_of(side * rows, rows), rows)],
            dst_ref=early_buf.at[index],
            send_sem=early_sem.at[0, index],
            recv_sem=early_sem.at[1, index],
            device_id={"col": mirror},
            device_id_type=MESH,
        )

    def gram_chunk(index, carry):
        cross_copy(index).wait_recv()
        write_both(index).start()
        total, cross = gram_update(both_buf[index])
        gram_buf[...] += total
        cross_buf[...] += cross
        return carry

    lax.fori_loop(0, half - 1, gram_chunk, 0)
    early_copy(0).start()
    gram_chunk(half - 1, 0)
    gram = gram_buf[...] + cross_buf[...].T
    quarter = rows // 2
    place = 0
    for i in range(4):
        for j in range(i + 1):
            tri_buf[place * quarter:(place + 1) * quarter, :] = gram[
                i * quarter:(i + 1) * quarter, j * quarter:(j + 1) * quarter
            ]
            place += 1

    size = parts.shape[1]

    def piece(index):
        return pl.ds(pl.multiple_of(index * size, size), size)

    def part_copy(step):
        return pltpu.make_async_remote_copy(
            src_ref=tri_buf.at[piece(lax.rem(ring + step, count))],
            dst_ref=parts.at[ring],
            send_sem=sum_sem.at[0],
            recv_sem=sum_sem.at[1],
            device_id=ring_device(step),
            device_id_type=MESH,
        )

    def total_copy(step):
        return pltpu.make_async_remote_copy(
            src_ref=total.at[ring],
            dst_ref=total.at[ring],
            send_sem=sum_sem.at[2],
            recv_sem=sum_sem.at[3],
            device_id=ring_device(step),
            device_id_type=MESH,
        )

    for step in range(1, count):
        part_copy(step).start()
    early_copy(1).start()
    parts[ring] = tri_buf[piece(ring), :]
    pieces = parts.at[pl.ds(0, count - 1)]
    pltpu.make_async_copy(pieces, pieces, sum_sem.at[1]).wait()
    value = parts[0]
    for index in range(1, count):
        value = value + parts[index]
    total[ring] = value
    for step in range(1, count):
        total_copy(step).start()
    early_copy(2).start()
    pltpu.make_async_copy(pieces, pieces, sum_sem.at[3]).wait()
    tri_ref[...] = total[...].reshape(tri_ref.shape)
    pltpu.make_async_copy(pieces, pieces, sum_sem.at[0]).wait()
    pltpu.make_async_copy(pieces, pieces, sum_sem.at[2]).wait()

    def write_early(index):
        return pltpu.make_async_copy(early_buf.at[index], early_hbm.at[index], early_sem.at[2, index])

    for index in range(EARLY):
        early_copy(index).wait_recv()
        write_early(index).start()
    for index in range(EARLY):
        early_copy(index).wait_send()
        write_early(index).wait()

    note_copy.wait()
    note_ref[...] = note_in[...]
    pltpu.make_async_copy(several, several, place_sem.at[0]).wait()

    def finish(index, carry):
        cross_copy(index).wait_send()
        write_other(index).wait()
        write_both(index).wait()
        return carry

    lax.fori_loop(0, half, finish, 0)
    for index in range(half - EARLY):
        write_own(index).wait()

    def sent(index, carry):
        pltpu.make_async_copy(
            out_buf.at[index, pl.ds(0, peers - 1)], out_buf.at[index, pl.ds(0, peers - 1)], out_sem.at[index]
        ).wait()
        return carry

    lax.fori_loop(0, CHUNKS, sent, 0)


def exchange(x, slot_source, slot_place, row_slot, send_slot, peers, row_count):
    rows, columns = x.shape
    width = columns // CHUNKS
    half = CHUNKS // 2
    count = 2 * row_count
    slots = slot_source.shape[1] // peers
    any_space = pl.BlockSpec(memory_space=pl.ANY)
    vmem = pl.BlockSpec(memory_space=pltpu.VMEM)
    smem = pl.BlockSpec(memory_space=pltpu.SMEM)
    return pl.pallas_call(
        functools.partial(exchange_kernel, peers, row_count),
        out_shape=[
            jax.ShapeDtypeStruct((half - EARLY, rows, width), F32),
            jax.ShapeDtypeStruct((half, rows, width), F32),
            jax.ShapeDtypeStruct((half, 2 * rows, width), F32),
            jax.ShapeDtypeStruct((EARLY, rows, width), F32),
            jax.ShapeDtypeStruct((10 * rows // 2, rows // 2), F32),
            jax.ShapeDtypeStruct((2, 8, rows), F32),
        ],
        in_specs=[vmem, vmem, vmem, vmem, smem],
        out_specs=[any_space, any_space, any_space, any_space, vmem, vmem],
        scratch_shapes=[
            pltpu.VMEM((CHUNKS, peers, slots, width), F32),
            pltpu.VMEM((CHUNKS, peers, slots, width), F32),
            pltpu.VMEM((half, 2 * rows, width), F32),
            pltpu.VMEM((half, rows, width), F32),
            pltpu.VMEM((EARLY, rows, width), F32),
            pltpu.VMEM((2 * rows, 2 * rows), F32),
            pltpu.VMEM((2 * rows, 2 * rows), F32),
            pltpu.VMEM((peers, slots, 128), F32),
            pltpu.VMEM((peers, slots, 128), F32),
            pltpu.VMEM((8, rows), F32),
            pltpu.VMEM((2, 8, rows), F32),
            pltpu.VMEM((10 * rows // 2, rows // 2), F32),
            pltpu.VMEM((count, 5 * rows // count, rows // 2), F32),
            pltpu.VMEM((count, 5 * rows // count, rows // 2), F32),
            pltpu.SemaphoreType.DMA((CHUNKS,)),
            pltpu.SemaphoreType.DMA((CHUNKS,)),
            pltpu.SemaphoreType.DMA((half,)),
            pltpu.SemaphoreType.DMA((half,)),
            pltpu.SemaphoreType.DMA((3 * half,)),
            pltpu.SemaphoreType.DMA((2,)),
            pltpu.SemaphoreType.DMA((2,)),
            pltpu.SemaphoreType.DMA((3, EARLY)),
            pltpu.SemaphoreType.DMA((4,)),
        ],
        compiler_params=pltpu.CompilerParams(
            collective_id=0, has_side_effects=True, vmem_limit_bytes=56 << 20
        ),
        cost_estimate=pl.CostEstimate(flops=10**10, bytes_accessed=10**8, transcendentals=0),
        name="exchange",
    )(x, slot_source, slot_place, row_slot, send_slot)


def inverse_factors(blocks):
    size = BLOCK
    groups = size // 8
    sublane = lax.broadcasted_iota(jnp.int32, (8, 2 * size), 0)
    lane = lax.broadcasted_iota(jnp.int32, (8, 2 * size), 1)
    held = []
    for block in blocks:
        parts = []
        for g in range(groups):
            unit = (lane == sublane + (size + 8 * g)).astype(F32)
            left = jnp.concatenate([block[8 * g:8 * g + 8, :], jnp.zeros((8, size), F32)], axis=1)
            parts.append(left + unit)
        held.append(parts)
    pivots = 8
    wide = (8, 2 * size)
    for j in range(0, size, pivots):
        first, within = divmod(j, 8)
        for parts in held:
            top = [jnp.broadcast_to(parts[first][within + k:within + k + 1, :], wide) for k in range(pivots)]
            pivot = [
                [jnp.broadcast_to(top[k][:, j + m:j + m + 1], wide) for m in range(pivots)] for k in range(pivots)
            ]
            columns = [
                [jnp.broadcast_to(parts[g][:, j + k:j + k + 1], wide) for g in range(first, groups)]
                for k in range(pivots)
            ]
            scaled = []
            for k in range(pivots):
                inverse = 1.0 / pivot[k][k]
                for m in range(k + 1, pivots):
                    factor = pivot[k][m] * inverse
                    for n in range(m, pivots):
                        pivot[m][n] = pivot[m][n] - factor * pivot[k][n]
                    top[m] = top[m] - factor * top[k]
                    columns[m] = [c - factor * d for c, d in zip(columns[m], columns[k])]
                scaled.append(top[k] * inverse)
            for g in range(first, groups):
                value = parts[g]
                for k in range(pivots):
                    value = value - columns[k][g - first] * scaled[k]
                if g == first:
                    value = jnp.where(sublane >= within + pivots, value, parts[g])
                    for k in range(pivots):
                        value = jnp.where(sublane == within + k, top[k], value)
                parts[g] = value
    result = []
    for parts in held:
        rows = []
        for g in range(groups):
            pivot = jnp.sum(jnp.where(lane == sublane + 8 * g, parts[g], 0.0), axis=1, keepdims=True)
            rows.append(parts[g] * lax.rsqrt(pivot))
        result.append(jnp.concatenate(rows, axis=0)[:, size:])
    return result


def eliminate(work_refs, width):
    size = work_refs[0].shape[0]
    for start in range(0, size, BLOCK):
        stop = start + BLOCK
        inverses = inverse_factors([work[start:stop, start:stop] for work in work_refs])
        base = start - start % 128
        for work, inverse in zip(work_refs, inverses):
            top = dot_f32(inverse, work[start:stop, base:width])
            work[start:stop, base:width] = top
            if stop < size:
                below = top[:, stop - base:size - base]
                work[stop:size, base:width] = work[stop:size, base:width] - dot_f32(below, top, ((0,), (0,)))


def orthogonal_steps(grams, work_refs):
    size = grams[0].shape[0]
    row = lax.broadcasted_iota(jnp.int32, (size, size), 0)
    column = lax.broadcasted_iota(jnp.int32, (size, size), 1)
    for gram, work in zip(grams, work_refs):
        trace = jnp.sum(jnp.where(row == column, gram, 0.0))
        gram = gram * (size / trace)
        work[:, :size] = dot_f32(gram, gram)
    eliminate(work_refs, size)
    for work in work_refs:
        factor = jnp.where(row <= column, work[:, :size], 0.0)
        work[:, :size] = dot_f32(factor, factor, ((1,), (1,)))
        work[:, size:] = factor
    eliminate(work_refs, 2 * size)
    return [work[:, size:] for work in work_refs]


def rotation_kernel(tri_ref, note_ref, side_ref, weight_ref, gram_buf, work_a, work_b):
    quarter = tri_ref.shape[1]
    size = 2 * quarter
    place = 0
    for i in range(4):
        for j in range(i + 1):
            block = tri_ref[place * quarter:(place + 1) * quarter, :]
            gram_buf[i * quarter:(i + 1) * quarter, j * quarter:(j + 1) * quarter] = block
            if i != j:
                gram_buf[j * quarter:(j + 1) * quarter, i * quarter:(i + 1) * quarter] = block.T
            place += 1
    side = side_ref[0]
    position = jnp.concatenate([note_ref[0, :1], note_ref[1, :1]], axis=1)
    slot = lax.broadcasted_iota(jnp.int32, (2 * size, 2 * size), 0)
    slot = jnp.where(side == 0, slot, (slot + size) % (2 * size))
    place_of = (slot.astype(F32) == position).astype(BF16)
    own_slot = note_ref[side, 1:2, :1]
    partner_slot = note_ref[1 - side, 1:2, :1]
    half_way = select_rows(place_of, gram_buf[...])
    gram_buf[...] = select_rows(place_of, half_way.T)
    own = gram_buf[:size, :size]
    partner = gram_buf[size:, size:]
    between = gram_buf[:size, size:]
    own_turn, partner_turn = orthogonal_steps([own, partner], [work_a, work_b])
    own_part = jnp.where(own_slot == 0, own_turn[quarter:], own_turn[:quarter])
    partner_part = jnp.where(partner_slot == 0, partner_turn[:quarter], partner_turn[quarter:])
    nt = ((1,), (1,))
    upper = dot_f32(dot_f32(own_part, own), own_part, nt)
    lower = dot_f32(dot_f32(partner_part, partner), partner_part, nt)
    mixed = dot_f32(dot_f32(own_part, between), partner_part, nt)
    gram_buf[:quarter, :quarter] = upper
    gram_buf[quarter:size, quarter:size] = lower
    gram_buf[:quarter, quarter:size] = mixed
    gram_buf[quarter:size, :quarter] = mixed.T
    second = gram_buf[:size, :size]
    (last,) = orthogonal_steps([0.5 * (second + second.T)], [work_a])
    gram_buf[:size, :size] = dot_f32(last[:, :quarter], own_part)
    gram_buf[:size, size:] = dot_f32(last[:, quarter:], partner_part)
    high, middle, low = split3(gram_buf[:size, :])
    dot = functools.partial(jnp.dot, preferred_element_type=F32)
    weight_ref[...] = (dot(high, place_of) + dot(middle, place_of)) + dot(low, place_of)


def rotations(tri, note, side):
    size = 2 * tri.shape[1]
    vmem = pl.BlockSpec(memory_space=pltpu.VMEM)
    smem = pl.BlockSpec(memory_space=pltpu.SMEM)
    return pl.pallas_call(
        rotation_kernel,
        out_shape=jax.ShapeDtypeStruct((size, 2 * size), F32),
        in_specs=[vmem, vmem, smem],
        out_specs=vmem,
        scratch_shapes=[
            pltpu.VMEM((2 * size, 2 * size), F32),
            pltpu.VMEM((size, 2 * size), F32),
            pltpu.VMEM((size, 2 * size), F32),
        ],
        compiler_params=pltpu.CompilerParams(vmem_limit_bytes=32 << 20),
        cost_estimate=pl.CostEstimate(flops=6 * 10**10, bytes_accessed=10**8, transcendentals=0),
        name="rotations",
    )(tri, note, side)


def product3(a, b):
    a_high = a.astype(BF16)
    a_low = (a - a_high.astype(F32)).astype(BF16)
    b_high = b.astype(BF16)
    b_low = (b - b_high.astype(F32)).astype(BF16)
    dot = functools.partial(jnp.dot, preferred_element_type=F32)
    return dot(a_high, b_high) + (dot(a_high, b_low) + dot(a_low, b_high))


def apply_both_kernel(start_ref, weight_ref, both_ref, out_ref):
    out_ref[...] = product3(weight_ref[...], both_ref[0])


def apply_both(start, weight, both, columns):
    chunks, rows, width = both.shape
    size = weight.shape[0]
    return pl.pallas_call(
        apply_both_kernel,
        grid_spec=pltpu.PrefetchScalarGridSpec(
            num_scalar_prefetch=1,
            grid=(chunks,),
            in_specs=[
                pl.BlockSpec((size, rows), lambda i, s: (0, 0)),
                pl.BlockSpec((1, rows, width), lambda i, s: (i, 0, 0)),
            ],
            out_specs=pl.BlockSpec((size, width), lambda i, s: (0, s[0] * chunks + i)),
        ),
        out_shape=jax.ShapeDtypeStruct((size, columns), F32),
        cost_estimate=pl.CostEstimate(flops=10**10, bytes_accessed=10**7, transcendentals=0),
        compiler_params=pltpu.CompilerParams(vmem_limit_bytes=32 << 20),
        name="apply_both",
    )(start, weight, both)


def apply_rest_kernel(start_ref, weight_ref, own_ref, early_ref, mirror_ref, partial_ref, out_ref):
    rows = own_ref.shape[1]
    side = start_ref[0]
    own_weight = jnp.where(side == 0, weight_ref[:, :rows], weight_ref[:, rows:])
    mirror_weight = jnp.where(side == 0, weight_ref[:, rows:], weight_ref[:, :rows])
    crossed = jnp.where(pl.program_id(0) < EARLY, early_ref[0], mirror_ref[0])
    out_ref[...] = product3(own_weight, own_ref[0]) + product3(mirror_weight, crossed)


def apply_rest(start, weight, own, early, mirror, partial):
    chunks, rows, width = own.shape
    size = weight.shape[0]
    return pl.pallas_call(
        apply_rest_kernel,
        grid_spec=pltpu.PrefetchScalarGridSpec(
            num_scalar_prefetch=1,
            grid=(chunks,),
            in_specs=[
                pl.BlockSpec((size, 2 * rows), lambda i, s: (0, 0)),
                pl.BlockSpec((1, rows, width), lambda i, s: (i, 0, 0)),
                pl.BlockSpec((1, rows, width), lambda i, s: (jnp.minimum(i, EARLY - 1), 0, 0)),
                pl.BlockSpec((1, rows, width), lambda i, s: (jnp.maximum(i - EARLY, 0), 0, 0)),
                pl.BlockSpec(memory_space=pl.ANY),
            ],
            out_specs=pl.BlockSpec((size, width), lambda i, s: (0, (1 - s[0]) * chunks + i)),
        ),
        out_shape=jax.ShapeDtypeStruct(partial.shape, F32),
        input_output_aliases={5: 0},
        cost_estimate=pl.CostEstimate(flops=10**10, bytes_accessed=10**7, transcendentals=0),
        compiler_params=pltpu.CompilerParams(vmem_limit_bytes=32 << 20),
        name="apply_rest",
    )(start, weight, own, early, mirror, partial)


def slot_tables(dest_ids, col, peers, slots):
    rows = dest_ids.shape[0]
    count = 2 * peers
    local = jnp.arange(rows, dtype=jnp.int32)
    target = dest_ids // rows
    peer = target % peers
    earlier = (peer[:, None] == peer[None, :]) & (local[None, :] < local[:, None])
    rank = jnp.sum(earlier.astype(jnp.int32), axis=1)
    wanted = jnp.arange(peers * slots, dtype=jnp.int32)
    slot = peer * slots + rank
    place = target // peers * rows + dest_ids % rows
    both = jnp.max(jnp.where(slot[None, :] == wanted[:, None], (place * rows + local)[None, :], -1), axis=1)
    slot_source = jnp.where(both < 0, -1, both % rows)
    slot_place = both // rows
    offset = (target - col) % peers
    amount = jnp.sum((offset[None, :] == jnp.arange(peers, dtype=jnp.int32)[:, None]).astype(jnp.int32), axis=1)
    sender = jnp.arange(peers, dtype=jnp.int32)
    sender_offset = (col - sender) % peers
    from_sender = jnp.sum(
        jnp.where(sender_offset[:, None] == jnp.arange(peers, dtype=jnp.int32)[None, :], amount[None, :], 0), axis=1
    )
    base = jnp.sum(jnp.where(sender[None, :] < sender[:, None], from_sender[None, :], 0), axis=1)
    within = jnp.arange(slots, dtype=jnp.int32)
    row_of_slot = jnp.where(within[None, :] < from_sender[:, None], base[:, None] + within[None, :], -1).reshape(-1)
    row_slot = jnp.max(jnp.where(row_of_slot[None, :] == local[:, None], wanted[None, :], -1), axis=1)
    return slot_source[None, :], slot_place[None, :], row_slot[None, :]


def body(row_count, greens_matrix, dest_ids, send_slot):
    rows, columns = greens_matrix.shape
    count = lax.axis_size("col")
    peers = count // 2
    cap = max(2, 2 * rows // count)
    slots = 2 * cap
    col = lax.axis_index("col")
    side = (col // peers).astype(jnp.int32)[None]
    slot_source, slot_place, row_slot = slot_tables(dest_ids, col, peers, slots)
    own, other, both, early, tri, note = exchange(
        greens_matrix, slot_source, slot_place, row_slot, send_slot, peers, row_count
    )
    mirror = lax.ppermute(own, "col", [(i, i ^ peers) for i in range(count)])
    weight = rotations(tri, note, side)
    partial = apply_both(side, weight, both, columns)
    return apply_rest(side, weight, other, early, mirror, partial)


def solution(mesh):
    return jax.shard_map(
        functools.partial(body, mesh.shape["row"]),
        mesh=mesh,
        in_specs=(P("col", "row"), P("col"), P("col")),
        out_specs=P("col", "row"),
        check_vma=False,
    )
```

```python
import functools

import jax
import jax.numpy as jnp
from jax import lax
from jax.experimental import pallas as pl
from jax.experimental.pallas import tpu as pltpu
from jax.sharding import PartitionSpec as P

CHUNKS = 16
EARLY = 2
TOGETHER = 2
BLOCK = 64
F32 = jnp.float32
BF16 = jnp.bfloat16
MESH = pl.DeviceIdType.MESH
HIGHEST = lax.Precision.HIGHEST


def split3(value):
    high = value.astype(BF16)
    rest = value - high.astype(F32)
    middle = rest.astype(BF16)
    low = (rest - middle.astype(F32)).astype(BF16)
    return high, middle, low


def select_rows(one_hot, value):
    high, middle, low = split3(value)
    dot = functools.partial(jnp.dot, one_hot, preferred_element_type=F32)
    return (dot(high) + dot(middle)) + dot(low)


def dot_f32(a, b, dims=((1,), (0,))):
    return lax.dot_general(a, b, (dims, ((), ())), precision=HIGHEST, preferred_element_type=F32)


def gram_update(rows):
    high, middle, low = split3(rows)
    nt = (((1,), (1,)), ((), ()))
    dot = functools.partial(lax.dot_general, dimension_numbers=nt, preferred_element_type=F32)
    cross = dot(middle, high) + dot(low, high)
    return dot(high, high) + dot(middle, middle) + cross, cross


def exchange_kernel(
    peers, row_count, x_hbm, row_slot_ref, row_place_ref, slot_row_ref, send_slot_ref,
    own_hbm, other_hbm, both_hbm, early_hbm, tri_ref, note_ref,
    x_buf, out_buf, in_buf, both_buf, other_buf, early_buf, gram_buf, cross_buf, place_out, place_in, note_out, note_in,
    tri_buf, parts, total,
    x_sem, out_sem, in_sem, z_out_sem, z_in_sem, write_sem, place_sem, note_sem, early_sem, sum_sem,
):
    col = lax.axis_index("col")
    side = col // peers
    me = col % peers
    mirror = lax.rem(col + peers, 2 * peers)
    half = CHUNKS // 2
    slots = out_buf.shape[2]
    width = out_buf.shape[3]
    rows = other_buf.shape[1]

    def read_chunk(index):
        chunk = lax.rem((1 - side) * half + index, CHUNKS)
        piece = x_hbm.at[:, pl.ds(pl.multiple_of(chunk * width, width), width)]
        return pltpu.make_async_copy(piece, x_buf.at[index], x_sem.at[index])

    def start_read(index, carry):
        read_chunk(index).start()
        return carry

    lax.fori_loop(0, CHUNKS, start_read, 0)
    barrier = pltpu.get_barrier_semaphore()

    def greet(step, carry):
        peer = side * peers + lax.rem(me + step, peers)
        pl.semaphore_signal(barrier, inc=1, device_id={"col": peer}, device_id_type=MESH)
        return carry

    count = 2 * row_count
    ring = side * row_count + lax.axis_index("row")

    def ring_device(step):
        index = lax.rem(ring + step, count)
        return {"col": (index // row_count) * peers + me, "row": index % row_count}

    lax.fori_loop(1, peers, greet, 0)
    for step in range(1, count):
        pl.semaphore_signal(barrier, inc=1, device_id=ring_device(step), device_id_type=MESH)
    pl.semaphore_wait(barrier, peers - 1 + count - 1)

    slot = lax.broadcasted_iota(jnp.int32, (peers * slots, rows), 0)
    pack = (row_slot_ref[...] == slot).astype(BF16)

    def send_chunk(index, carry):
        read_chunk(index).wait()
        out_buf[index] = select_rows(pack, x_buf[index]).reshape(peers, slots, width)

        def send(step, inner):
            peer = lax.rem(me + step, peers)
            pltpu.make_async_remote_copy(
                src_ref=out_buf.at[index, peer],
                dst_ref=in_buf.at[index, me],
                send_sem=out_sem.at[index],
                recv_sem=in_sem.at[index],
                device_id={"col": side * peers + peer},
                device_id_type=MESH,
            ).start()
            return inner

        lax.fori_loop(1, peers, send, 0)
        in_buf[index, me] = out_buf[index, me]
        return carry

    lax.fori_loop(0, CHUNKS, send_chunk, 0)

    places = jnp.broadcast_to(row_place_ref[...].astype(F32), (128, rows)).T
    place_out[...] = select_rows(pack, places).reshape(peers, slots, 128)

    def send_places(step, carry):
        peer = lax.rem(me + step, peers)
        pltpu.make_async_remote_copy(
            src_ref=place_out.at[peer],
            dst_ref=place_in.at[me],
            send_sem=place_sem.at[0],
            recv_sem=place_sem.at[1],
            device_id={"col": side * peers + peer},
            device_id_type=MESH,
        ).start()
        return carry

    lax.fori_loop(1, peers, send_places, 0)
    place_in[me] = place_out[me]

    place = lax.broadcasted_iota(jnp.int32, (rows, peers * slots), 0)
    compact = (slot_row_ref[...] == place).astype(BF16)

    def arrived(index):
        pltpu.make_async_copy(
            in_buf.at[index, pl.ds(0, peers - 1)], in_buf.at[index, pl.ds(0, peers - 1)], in_sem.at[index]
        ).wait()
        return select_rows(compact, in_buf[index].reshape(peers * slots, width))

    def cross_copy(index):
        return pltpu.make_async_remote_copy(
            src_ref=other_buf.at[index],
            dst_ref=both_buf.at[index, pl.ds(pl.multiple_of(side * rows, rows), rows)],
            send_sem=z_out_sem.at[index],
            recv_sem=z_in_sem.at[index],
            device_id={"col": mirror},
            device_id_type=MESH,
        )

    def write_other(index):
        return pltpu.make_async_copy(other_buf.at[index], other_hbm.at[index], write_sem.at[index])

    def write_own(index):
        source = both_buf.at[EARLY + index, pl.ds(pl.multiple_of(side * rows, rows), rows)]
        return pltpu.make_async_copy(source, own_hbm.at[index], write_sem.at[half + index])

    def write_both(index):
        return pltpu.make_async_copy(both_buf.at[index], both_hbm.at[index], write_sem.at[2 * half + index])

    def cross_chunk(index, carry):
        other_buf[index] = arrived(index)
        cross_copy(index).start()
        write_other(index).start()
        return carry

    lax.fori_loop(0, half, cross_chunk, 0)

    def keep_chunk(index, carry):
        both_buf[index, pl.ds(pl.multiple_of(side * rows, rows), rows)] = arrived(half + index)
        return carry

    lax.fori_loop(0, half, keep_chunk, 0)
    for index in range(half - EARLY):
        write_own(index).start()

    several = place_in.at[pl.ds(0, peers - 1)]
    pltpu.make_async_copy(several, several, place_sem.at[1]).wait()
    listed = select_rows(compact, place_in[...].reshape(peers * slots, 128)).T[:8]
    first_row = lax.broadcasted_iota(jnp.int32, listed.shape, 0) == 0
    note_out[...] = jnp.where(first_row, listed, send_slot_ref[0].astype(F32))
    note_in[side] = note_out[...]
    note_copy = pltpu.make_async_remote_copy(
        src_ref=note_out,
        dst_ref=note_in.at[side],
        send_sem=note_sem.at[0],
        recv_sem=note_sem.at[1],
        device_id={"col": mirror},
        device_id_type=MESH,
    )
    note_copy.start()

    gram_buf[...] = jnp.zeros_like(gram_buf)
    cross_buf[...] = jnp.zeros_like(cross_buf)

    def early_copy(index):
        return pltpu.make_async_remote_copy(
            src_ref=both_buf.at[index, pl.ds(pl.multiple_of(side * rows, rows), rows)],
            dst_ref=early_buf.at[index],
            send_sem=early_sem.at[0, index],
            recv_sem=early_sem.at[1, index],
            device_id={"col": mirror},
            device_id_type=MESH,
        )

    def gram_chunk(index, carry):
        cross_copy(index).wait_recv()
        write_both(index).start()
        total, cross = gram_update(both_buf[index])
        gram_buf[...] += total
        cross_buf[...] += cross
        return carry

    lax.fori_loop(0, half - 1, gram_chunk, 0)
    early_copy(0).start()
    gram_chunk(half - 1, 0)
    gram = gram_buf[...] + cross_buf[...].T
    quarter = rows // 2
    place = 0
    for i in range(4):
        for j in range(i + 1):
            tri_buf[place * quarter:(place + 1) * quarter, :] = gram[
                i * quarter:(i + 1) * quarter, j * quarter:(j + 1) * quarter
            ]
            place += 1

    size = parts.shape[1]

    def piece(index):
        return pl.ds(pl.multiple_of(index * size, size), size)

    def part_copy(step):
        return pltpu.make_async_remote_copy(
            src_ref=tri_buf.at[piece(lax.rem(ring + step, count))],
            dst_ref=parts.at[ring],
            send_sem=sum_sem.at[0],
            recv_sem=sum_sem.at[1],
            device_id=ring_device(step),
            device_id_type=MESH,
        )

    def total_copy(step):
        return pltpu.make_async_remote_copy(
            src_ref=total.at[ring],
            dst_ref=total.at[ring],
            send_sem=sum_sem.at[2],
            recv_sem=sum_sem.at[3],
            device_id=ring_device(step),
            device_id_type=MESH,
        )

    for step in range(1, count):
        part_copy(step).start()
    early_copy(1).start()
    parts[ring] = tri_buf[piece(ring), :]
    pieces = parts.at[pl.ds(0, count - 1)]
    pltpu.make_async_copy(pieces, pieces, sum_sem.at[1]).wait()
    value = parts[0]
    for index in range(1, count):
        value = value + parts[index]
    total[ring] = value
    for step in range(1, count):
        total_copy(step).start()
    pltpu.make_async_copy(pieces, pieces, sum_sem.at[3]).wait()
    tri_ref[...] = total[...].reshape(tri_ref.shape)
    pltpu.make_async_copy(pieces, pieces, sum_sem.at[0]).wait()
    pltpu.make_async_copy(pieces, pieces, sum_sem.at[2]).wait()

    def write_early(index):
        return pltpu.make_async_copy(early_buf.at[index], early_hbm.at[index], early_sem.at[2, index])

    for index in range(EARLY):
        early_copy(index).wait_recv()
        write_early(index).start()
    for index in range(EARLY):
        early_copy(index).wait_send()
        write_early(index).wait()

    note_copy.wait()
    note_ref[...] = note_in[...]
    pltpu.make_async_copy(several, several, place_sem.at[0]).wait()

    def finish(index, carry):
        cross_copy(index).wait_send()
        write_other(index).wait()
        write_both(index).wait()
        return carry

    lax.fori_loop(0, half, finish, 0)
    for index in range(half - EARLY):
        write_own(index).wait()

    def sent(index, carry):
        pltpu.make_async_copy(
            out_buf.at[index, pl.ds(0, peers - 1)], out_buf.at[index, pl.ds(0, peers - 1)], out_sem.at[index]
        ).wait()
        return carry

    lax.fori_loop(0, CHUNKS, sent, 0)


def exchange(x, row_slot, row_place, slot_row, send_slot, peers, row_count):
    rows, columns = x.shape
    width = columns // CHUNKS
    half = CHUNKS // 2
    count = 2 * row_count
    slots = slot_row.shape[1] // peers
    any_space = pl.BlockSpec(memory_space=pl.ANY)
    vmem = pl.BlockSpec(memory_space=pltpu.VMEM)
    smem = pl.BlockSpec(memory_space=pltpu.SMEM)
    return pl.pallas_call(
        functools.partial(exchange_kernel, peers, row_count),
        out_shape=[
            jax.ShapeDtypeStruct((half - EARLY, rows, width), F32),
            jax.ShapeDtypeStruct((half, rows, width), F32),
            jax.ShapeDtypeStruct((half, 2 * rows, width), F32),
            jax.ShapeDtypeStruct((EARLY, rows, width), F32),
            jax.ShapeDtypeStruct((10 * rows // 2, rows // 2), F32),
            jax.ShapeDtypeStruct((2, 8, rows), F32),
        ],
        in_specs=[any_space, vmem, vmem, vmem, smem],
        out_specs=[any_space, any_space, any_space, any_space, vmem, vmem],
        scratch_shapes=[
            pltpu.VMEM((CHUNKS, rows, width), F32),
            pltpu.VMEM((CHUNKS, peers, slots, width), F32),
            pltpu.VMEM((CHUNKS, peers, slots, width), F32),
            pltpu.VMEM((half, 2 * rows, width), F32),
            pltpu.VMEM((half, rows, width), F32),
            pltpu.VMEM((EARLY, rows, width), F32),
            pltpu.VMEM((2 * rows, 2 * rows), F32),
            pltpu.VMEM((2 * rows, 2 * rows), F32),
            pltpu.VMEM((peers, slots, 128), F32),
            pltpu.VMEM((peers, slots, 128), F32),
            pltpu.VMEM((8, rows), F32),
            pltpu.VMEM((2, 8, rows), F32),
            pltpu.VMEM((10 * rows // 2, rows // 2), F32),
            pltpu.VMEM((count, 5 * rows // count, rows // 2), F32),
            pltpu.VMEM((count, 5 * rows // count, rows // 2), F32),
            pltpu.SemaphoreType.DMA((CHUNKS,)),
            pltpu.SemaphoreType.DMA((CHUNKS,)),
            pltpu.SemaphoreType.DMA((CHUNKS,)),
            pltpu.SemaphoreType.DMA((half,)),
            pltpu.SemaphoreType.DMA((half,)),
            pltpu.SemaphoreType.DMA((3 * half,)),
            pltpu.SemaphoreType.DMA((2,)),
            pltpu.SemaphoreType.DMA((2,)),
            pltpu.SemaphoreType.DMA((3, EARLY)),
            pltpu.SemaphoreType.DMA((4,)),
        ],
        compiler_params=pltpu.CompilerParams(
            collective_id=0, has_side_effects=True, vmem_limit_bytes=56 << 20
        ),
        cost_estimate=pl.CostEstimate(flops=10**10, bytes_accessed=10**8, transcendentals=0),
        name="exchange",
    )(x, row_slot, row_place, slot_row, send_slot)


def inverse_factors(blocks):
    size = BLOCK
    groups = size // 8
    sublane = lax.broadcasted_iota(jnp.int32, (8, 2 * size), 0)
    lane = lax.broadcasted_iota(jnp.int32, (8, 2 * size), 1)
    held = []
    for block in blocks:
        parts = []
        for g in range(groups):
            unit = (lane == sublane + (size + 8 * g)).astype(F32)
            left = jnp.concatenate([block[8 * g:8 * g + 8, :], jnp.zeros((8, size), F32)], axis=1)
            parts.append(left + unit)
        held.append(parts)
    pivots = 8
    wide = (8, 2 * size)
    for j in range(0, size, pivots):
        first, within = divmod(j, 8)
        for parts in held:
            top = [jnp.broadcast_to(parts[first][within + k:within + k + 1, :], wide) for k in range(pivots)]
            pivot = [
                [jnp.broadcast_to(top[k][:, j + m:j + m + 1], wide) for m in range(pivots)] for k in range(pivots)
            ]
            columns = [
                [jnp.broadcast_to(parts[g][:, j + k:j + k + 1], wide) for g in range(first, groups)]
                for k in range(pivots)
            ]
            scaled = []
            for k in range(pivots):
                inverse = 1.0 / pivot[k][k]
                for m in range(k + 1, pivots):
                    factor = pivot[k][m] * inverse
                    for n in range(m, pivots):
                        pivot[m][n] = pivot[m][n] - factor * pivot[k][n]
                    top[m] = top[m] - factor * top[k]
                    columns[m] = [c - factor * d for c, d in zip(columns[m], columns[k])]
                scaled.append(top[k] * inverse)
            for g in range(first, groups):
                value = parts[g]
                for k in range(pivots):
                    value = value - columns[k][g - first] * scaled[k]
                if g == first:
                    value = jnp.where(sublane >= within + pivots, value, parts[g])
                    for k in range(pivots):
                        value = jnp.where(sublane == within + k, top[k], value)
                parts[g] = value
    result = []
    for parts in held:
        rows = []
        for g in range(groups):
            pivot = jnp.sum(jnp.where(lane == sublane + 8 * g, parts[g], 0.0), axis=1, keepdims=True)
            rows.append(parts[g] * lax.rsqrt(pivot))
        result.append(jnp.concatenate(rows, axis=0)[:, size:])
    return result


def eliminate(work_refs, width):
    size = work_refs[0].shape[0]
    for start in range(0, size, BLOCK):
        stop = start + BLOCK
        inverses = inverse_factors([work[start:stop, start:stop] for work in work_refs])
        base = start - start % 128
        for work, inverse in zip(work_refs, inverses):
            top = dot_f32(inverse, work[start:stop, base:width])
            work[start:stop, base:width] = top
            if stop < size:
                below = top[:, stop - base:size - base]
                work[stop:size, base:width] = work[stop:size, base:width] - dot_f32(below, top, ((0,), (0,)))


def orthogonal_steps(grams, work_refs):
    size = grams[0].shape[0]
    row = lax.broadcasted_iota(jnp.int32, (size, size), 0)
    column = lax.broadcasted_iota(jnp.int32, (size, size), 1)
    for gram, work in zip(grams, work_refs):
        trace = jnp.sum(jnp.where(row == column, gram, 0.0))
        gram = gram * (size / trace)
        work[:, :size] = dot_f32(gram, gram)
    eliminate(work_refs, size)
    for work in work_refs:
        factor = jnp.where(row <= column, work[:, :size], 0.0)
        work[:, :size] = dot_f32(factor, factor, ((1,), (1,)))
        work[:, size:] = factor
    eliminate(work_refs, 2 * size)
    return [work[:, size:] for work in work_refs]


def rotation_kernel(tri_ref, note_ref, side_ref, high_ref, low_ref, gram_buf, work_a, work_b):
    quarter = tri_ref.shape[1]
    size = 2 * quarter
    place = 0
    for i in range(4):
        for j in range(i + 1):
            block = tri_ref[place * quarter:(place + 1) * quarter, :]
            gram_buf[i * quarter:(i + 1) * quarter, j * quarter:(j + 1) * quarter] = block
            if i != j:
                gram_buf[j * quarter:(j + 1) * quarter, i * quarter:(i + 1) * quarter] = block.T
            place += 1
    side = side_ref[0]
    position = jnp.concatenate([note_ref[0, :1], note_ref[1, :1]], axis=1)
    slot = lax.broadcasted_iota(jnp.int32, (2 * size, 2 * size), 0)
    slot = jnp.where(side == 0, slot, (slot + size) % (2 * size))
    place_of = (slot.astype(F32) == position).astype(BF16)
    own_slot = note_ref[side, 1:2, :1]
    partner_slot = note_ref[1 - side, 1:2, :1]
    half_way = select_rows(place_of, gram_buf[...])
    gram_buf[...] = select_rows(place_of, half_way.T)
    own = gram_buf[:size, :size]
    partner = gram_buf[size:, size:]
    between = gram_buf[:size, size:]
    own_turn, partner_turn = orthogonal_steps([own, partner], [work_a, work_b])
    own_part = jnp.where(own_slot == 0, own_turn[quarter:], own_turn[:quarter])
    partner_part = jnp.where(partner_slot == 0, partner_turn[:quarter], partner_turn[quarter:])
    nt = ((1,), (1,))
    upper = dot_f32(dot_f32(own_part, own), own_part, nt)
    lower = dot_f32(dot_f32(partner_part, partner), partner_part, nt)
    mixed = dot_f32(dot_f32(own_part, between), partner_part, nt)
    gram_buf[:quarter, :quarter] = upper
    gram_buf[quarter:size, quarter:size] = lower
    gram_buf[:quarter, quarter:size] = mixed
    gram_buf[quarter:size, :quarter] = mixed.T
    second = gram_buf[:size, :size]
    (last,) = orthogonal_steps([0.5 * (second + second.T)], [work_a])
    gram_buf[:size, :size] = dot_f32(last[:, :quarter], own_part)
    gram_buf[:size, size:] = dot_f32(last[:, quarter:], partner_part)
    high, middle, low = split3(gram_buf[:size, :])
    dot = functools.partial(jnp.dot, preferred_element_type=F32)
    weight = (dot(high, place_of) + dot(middle, place_of)) + dot(low, place_of)
    high = weight.astype(BF16)
    high_ref[...] = high
    low_ref[...] = (weight - high.astype(F32)).astype(BF16)


def rotations(tri, note, side):
    size = 2 * tri.shape[1]
    vmem = pl.BlockSpec(memory_space=pltpu.VMEM)
    smem = pl.BlockSpec(memory_space=pltpu.SMEM)
    return pl.pallas_call(
        rotation_kernel,
        out_shape=[jax.ShapeDtypeStruct((size, 2 * size), BF16)] * 2,
        in_specs=[vmem, vmem, smem],
        out_specs=[vmem, vmem],
        scratch_shapes=[
            pltpu.VMEM((2 * size, 2 * size), F32),
            pltpu.VMEM((size, 2 * size), F32),
            pltpu.VMEM((size, 2 * size), F32),
        ],
        compiler_params=pltpu.CompilerParams(vmem_limit_bytes=32 << 20),
        cost_estimate=pl.CostEstimate(flops=6 * 10**10, bytes_accessed=10**8, transcendentals=0),
        name="rotations",
    )(tri, note, side)


def product3(a_high, a_low, b):
    b_high = b.astype(BF16)
    b_low = (b - b_high.astype(F32)).astype(BF16)
    dot = functools.partial(jnp.dot, preferred_element_type=F32)
    return dot(a_high, b_high) + (dot(a_high, b_low) + dot(a_low, b_high))


def apply_both_kernel(side_ref, high_ref, low_ref, both_ref, out_ref):
    width = both_ref.shape[2]
    for k in range(TOGETHER):
        out_ref[:, k * width:(k + 1) * width] = product3(high_ref[...], low_ref[...], both_ref[k])


def apply_both(side, high, low, both, columns):
    chunks, rows, width = both.shape
    size = high.shape[0]
    steps = chunks // TOGETHER
    weight = pl.BlockSpec((size, rows), lambda i, s: (0, 0))
    return pl.pallas_call(
        apply_both_kernel,
        grid_spec=pltpu.PrefetchScalarGridSpec(
            num_scalar_prefetch=1,
            grid=(steps,),
            in_specs=[weight, weight, pl.BlockSpec((TOGETHER, rows, width), lambda i, s: (i, 0, 0))],
            out_specs=pl.BlockSpec((size, TOGETHER * width), lambda i, s: (0, s[0] * steps + i)),
        ),
        out_shape=jax.ShapeDtypeStruct((size, columns), F32),
        cost_estimate=pl.CostEstimate(flops=10**10, bytes_accessed=10**7, transcendentals=0),
        compiler_params=pltpu.CompilerParams(vmem_limit_bytes=32 << 20),
        name="apply_both",
    )(side, high, low, both)


def apply_rest_kernel(
    side_ref, high_ref, low_ref, mirror_high_ref, mirror_low_ref, own_ref, early_ref, mirror_ref, partial_ref, out_ref
):
    width = own_ref.shape[2]
    first = pl.program_id(0) == 0
    for k in range(TOGETHER):
        crossed = mirror_ref[k]
        if k < EARLY:
            crossed = jnp.where(first, early_ref[k], crossed)
        out_ref[:, k * width:(k + 1) * width] = product3(high_ref[...], low_ref[...], own_ref[k]) + product3(
            mirror_high_ref[...], mirror_low_ref[...], crossed
        )


def apply_rest(side, high, low, own, early, mirror, partial):
    chunks, rows, width = own.shape
    size = high.shape[0]
    steps = chunks // TOGETHER
    weight = pl.BlockSpec((size, rows), lambda i, s: (0, s[0]))
    mirror_weight = pl.BlockSpec((size, rows), lambda i, s: (0, 1 - s[0]))
    return pl.pallas_call(
        apply_rest_kernel,
        grid_spec=pltpu.PrefetchScalarGridSpec(
            num_scalar_prefetch=1,
            grid=(steps,),
            in_specs=[
                weight,
                weight,
                mirror_weight,
                mirror_weight,
                pl.BlockSpec((TOGETHER, rows, width), lambda i, s: (i, 0, 0)),
                pl.BlockSpec((EARLY, rows, width), lambda i, s: (0, 0, 0)),
                pl.BlockSpec((TOGETHER, rows, width), lambda i, s: (jnp.maximum(i - 1, 0), 0, 0)),
                pl.BlockSpec(memory_space=pl.ANY),
            ],
            out_specs=pl.BlockSpec((size, TOGETHER * width), lambda i, s: (0, (1 - s[0]) * steps + i)),
        ),
        out_shape=jax.ShapeDtypeStruct(partial.shape, F32),
        input_output_aliases={8: 0},
        cost_estimate=pl.CostEstimate(flops=10**10, bytes_accessed=10**7, transcendentals=0),
        compiler_params=pltpu.CompilerParams(vmem_limit_bytes=32 << 20),
        name="apply_rest",
    )(side, high, low, high, low, own, early, mirror, partial)


def slot_tables(dest_ids, col, peers, slots):
    rows = dest_ids.shape[0]
    count = 2 * peers
    local = jnp.arange(rows, dtype=jnp.int32)
    target = dest_ids // rows
    peer = target % peers
    earlier = (peer[:, None] == peer[None, :]) & (local[None, :] < local[:, None])
    rank = jnp.sum(earlier.astype(jnp.int32), axis=1)
    row_slot = peer * slots + rank
    row_place = target // peers * rows + dest_ids % rows
    offset = (target - col) % peers
    amount = jnp.sum((offset[None, :] == jnp.arange(peers, dtype=jnp.int32)[:, None]).astype(jnp.int32), axis=1)
    sender = jnp.arange(peers, dtype=jnp.int32)
    sender_offset = (col - sender) % peers
    from_sender = jnp.sum(
        jnp.where(sender_offset[:, None] == jnp.arange(peers, dtype=jnp.int32)[None, :], amount[None, :], 0), axis=1
    )
    base = jnp.sum(jnp.where(sender[None, :] < sender[:, None], from_sender[None, :], 0), axis=1)
    within = jnp.arange(slots, dtype=jnp.int32)
    slot_row = jnp.where(within[None, :] < from_sender[:, None], base[:, None] + within[None, :], -1).reshape(-1)
    return row_slot[None, :], row_place[None, :], slot_row[None, :]


def body(row_count, greens_matrix, dest_ids, send_slot):
    rows, columns = greens_matrix.shape
    count = lax.axis_size("col")
    peers = count // 2
    cap = max(2, 2 * rows // count)
    slots = 2 * cap
    col = lax.axis_index("col")
    side = (col // peers).astype(jnp.int32)[None]
    row_slot, row_place, slot_row = slot_tables(dest_ids, col, peers, slots)
    own, other, both, early, tri, note = exchange(
        greens_matrix, row_slot, row_place, slot_row, send_slot, peers, row_count
    )
    mirror = lax.ppermute(own, "col", [(i, i ^ peers) for i in range(count)])
    high, low = rotations(tri, note, side)
    partial = apply_both(side, high, low, both, columns)
    return apply_rest(side, high, low, other, early, mirror, partial)


def solution(mesh):
    return jax.shard_map(
        functools.partial(body, mesh.shape["row"]),
        mesh=mesh,
        in_specs=(P("col", "row"), P("col"), P("col")),
        out_specs=P("col", "row"),
        check_vma=False,
    )
```

```python
import functools

import jax
import jax.numpy as jnp
from jax import lax
from jax.experimental import pallas as pl
from jax.experimental.pallas import tpu as pltpu
from jax.sharding import PartitionSpec as P

CHUNKS = 16
EARLY = 2
TOGETHER = 2
LEAD = 3
BLOCK = 64
F32 = jnp.float32
BF16 = jnp.bfloat16
MESH = pl.DeviceIdType.MESH
HIGHEST = lax.Precision.HIGHEST


def split3(value):
    high = value.astype(BF16)
    rest = value - high.astype(F32)
    middle = rest.astype(BF16)
    low = (rest - middle.astype(F32)).astype(BF16)
    return high, middle, low


def select_rows(one_hot, value):
    high, middle, low = split3(value)
    dot = functools.partial(jnp.dot, one_hot, preferred_element_type=F32)
    return (dot(high) + dot(middle)) + dot(low)


def dot_f32(a, b, dims=((1,), (0,))):
    return lax.dot_general(a, b, (dims, ((), ())), precision=HIGHEST, preferred_element_type=F32)


def gram_update(rows):
    high, middle, low = split3(rows)
    nt = (((1,), (1,)), ((), ()))
    dot = functools.partial(lax.dot_general, dimension_numbers=nt, preferred_element_type=F32)
    cross = dot(middle, high) + dot(low, high)
    return dot(high, high) + dot(middle, middle) + cross, cross


def slot_tables(ids, col, peers, slots):
    rows = ids.shape[1]

    def log2(number):
        return number.bit_length() - 1

    def upright(values):
        return jnp.broadcast_to(values, (128, rows)).T[:, :1]

    target = lax.shift_right_logical(ids, log2(rows))
    peer = target & (peers - 1)
    row_place = (lax.shift_right_logical(target, log2(peers)) * rows + (ids & (rows - 1))).astype(F32)
    sender = upright(((col - ((target - col) & (peers - 1))) & (peers - 1)).astype(F32))
    peer = peer.astype(F32)
    earlier = lax.broadcasted_iota(jnp.int32, (rows, rows), 0) < lax.broadcasted_iota(jnp.int32, (rows, rows), 1)
    same = jnp.where(upright(peer) == peer, 1.0, 0.0)
    rank = jnp.sum(jnp.where(earlier, same, 0.0), axis=0, keepdims=True)
    slot = lax.broadcasted_iota(jnp.int32, (peers * slots, rows), 0).astype(F32)
    pack = (peer * slots + rank == slot).astype(BF16)
    incoming = lax.broadcasted_iota(jnp.int32, (rows, peers * slots), 1)
    origin = lax.shift_right_logical(incoming, log2(slots)).astype(F32)
    within = (incoming & (slots - 1))[:1].astype(F32)
    amount = jnp.sum(jnp.where(sender == origin, 1.0, 0.0), axis=0, keepdims=True)
    base = jnp.sum(jnp.where(sender < origin, 1.0, 0.0), axis=0, keepdims=True)
    wanted = jnp.where(within < amount, base + within, -1.0)
    place = lax.broadcasted_iota(jnp.int32, (rows, peers * slots), 0).astype(F32)
    return pack, (wanted == place).astype(BF16), row_place


def exchange_kernel(
    peers, row_count, slots, x_hbm, ids_ref, send_slot_ref,
    own_hbm, other_hbm, both_hbm, early_hbm, tri_ref, note_ref,
    x_buf, out_buf, in_buf, both_buf, other_buf, early_buf, gram_buf, cross_buf, place_out, place_in, note_out, note_in,
    tri_buf, parts, total,
    x_sem, out_sem, in_sem, z_out_sem, z_in_sem, write_sem, place_sem, note_sem, early_sem, sum_sem,
):
    col = lax.axis_index("col")
    side = col // peers
    me = col % peers
    mirror = lax.rem(col + peers, 2 * peers)
    half = CHUNKS // 2
    width = out_buf.shape[3]
    rows = other_buf.shape[1]

    def read_chunk(index):
        chunk = lax.rem((1 - side) * half + index, CHUNKS)
        piece = x_hbm.at[:, pl.ds(pl.multiple_of(chunk * width, width), width)]
        return pltpu.make_async_copy(piece, x_buf.at[index], x_sem.at[index])

    def start_read(index, carry):
        read_chunk(index).start()
        return carry

    lax.fori_loop(0, CHUNKS, start_read, 0)
    barrier = pltpu.get_barrier_semaphore()

    def greet(step, carry):
        peer = side * peers + lax.rem(me + step, peers)
        pl.semaphore_signal(barrier, inc=1, device_id={"col": peer}, device_id_type=MESH)
        return carry

    count = 2 * row_count
    ring = side * row_count + lax.axis_index("row")

    def ring_device(step):
        index = lax.rem(ring + step, count)
        return {"col": (index // row_count) * peers + me, "row": index % row_count}

    lax.fori_loop(1, peers, greet, 0)
    for step in range(1, count):
        pl.semaphore_signal(barrier, inc=1, device_id=ring_device(step), device_id_type=MESH)
    pl.semaphore_wait(barrier, peers - 1 + count - 1)

    pack, compact, row_place = slot_tables(ids_ref[...], col, peers, slots)

    def send_chunk(index, carry):
        read_chunk(index).wait()
        out_buf[index] = select_rows(pack, x_buf[index]).reshape(peers, slots, width)

        def send(step, inner):
            peer = lax.rem(me + step, peers)
            pltpu.make_async_remote_copy(
                src_ref=out_buf.at[index, peer],
                dst_ref=in_buf.at[index, me],
                send_sem=out_sem.at[index],
                recv_sem=in_sem.at[index],
                device_id={"col": side * peers + peer},
                device_id_type=MESH,
            ).start()
            return inner

        lax.fori_loop(1, peers, send, 0)
        in_buf[index, me] = out_buf[index, me]
        return carry

    def arrived(index):
        pltpu.make_async_copy(
            in_buf.at[index, pl.ds(0, peers - 1)], in_buf.at[index, pl.ds(0, peers - 1)], in_sem.at[index]
        ).wait()
        return select_rows(compact, in_buf[index].reshape(peers * slots, width))

    def cross_copy(index):
        return pltpu.make_async_remote_copy(
            src_ref=other_buf.at[index],
            dst_ref=both_buf.at[index, pl.ds(pl.multiple_of(side * rows, rows), rows)],
            send_sem=z_out_sem.at[index],
            recv_sem=z_in_sem.at[index],
            device_id={"col": mirror},
            device_id_type=MESH,
        )

    def write_other(index):
        return pltpu.make_async_copy(other_buf.at[index], other_hbm.at[index], write_sem.at[index])

    def write_own(index):
        source = both_buf.at[EARLY + index, pl.ds(pl.multiple_of(side * rows, rows), rows)]
        return pltpu.make_async_copy(source, own_hbm.at[index], write_sem.at[half + index])

    def write_both(index):
        return pltpu.make_async_copy(both_buf.at[index], both_hbm.at[index], write_sem.at[2 * half + index])

    def cross_chunk(index, carry):
        other_buf[index] = arrived(index)
        cross_copy(index).start()
        write_other(index).start()
        return carry

    def keep_chunk(index, carry):
        both_buf[index, pl.ds(pl.multiple_of(side * rows, rows), rows)] = arrived(half + index)
        return carry

    def send_and_cross(index, carry):
        send_chunk(index + LEAD, carry)
        return cross_chunk(index, carry)

    def send_and_keep(index, carry):
        send_chunk(half + index + LEAD, carry)
        return keep_chunk(index, carry)

    lax.fori_loop(0, LEAD, send_chunk, 0)
    lax.fori_loop(0, half, send_and_cross, 0)
    lax.fori_loop(0, half - LEAD, send_and_keep, 0)
    places = jnp.broadcast_to(row_place, (128, rows)).T
    place_out[...] = select_rows(pack, places).reshape(peers, slots, 128)

    def send_places(step, carry):
        peer = lax.rem(me + step, peers)
        pltpu.make_async_remote_copy(
            src_ref=place_out.at[peer],
            dst_ref=place_in.at[me],
            send_sem=place_sem.at[0],
            recv_sem=place_sem.at[1],
            device_id={"col": side * peers + peer},
            device_id_type=MESH,
        ).start()
        return carry

    lax.fori_loop(1, peers, send_places, 0)
    place_in[me] = place_out[me]

    lax.fori_loop(half - LEAD, half, keep_chunk, 0)
    for index in range(half - EARLY):
        write_own(index).start()

    several = place_in.at[pl.ds(0, peers - 1)]
    pltpu.make_async_copy(several, several, place_sem.at[1]).wait()
    listed = select_rows(compact, place_in[...].reshape(peers * slots, 128)).T[:8]
    first_row = lax.broadcasted_iota(jnp.int32, listed.shape, 0) == 0
    note_out[...] = jnp.where(first_row, listed, send_slot_ref[0].astype(F32))
    note_in[side] = note_out[...]
    note_copy = pltpu.make_async_remote_copy(
        src_ref=note_out,
        dst_ref=note_in.at[side],
        send_sem=note_sem.at[0],
        recv_sem=note_sem.at[1],
        device_id={"col": mirror},
        device_id_type=MESH,
    )
    note_copy.start()

    gram_buf[...] = jnp.zeros_like(gram_buf)
    cross_buf[...] = jnp.zeros_like(cross_buf)

    def early_copy(index):
        return pltpu.make_async_remote_copy(
            src_ref=both_buf.at[index, pl.ds(pl.multiple_of(side * rows, rows), rows)],
            dst_ref=early_buf.at[index],
            send_sem=early_sem.at[0, index],
            recv_sem=early_sem.at[1, index],
            device_id={"col": mirror},
            device_id_type=MESH,
        )

    def gram_chunk(index, carry):
        cross_copy(index).wait_recv()
        write_both(index).start()
        total, cross = gram_update(both_buf[index])
        gram_buf[...] += total
        cross_buf[...] += cross
        return carry

    lax.fori_loop(0, half - 1, gram_chunk, 0)
    early_copy(0).start()
    gram_chunk(half - 1, 0)
    gram = gram_buf[...] + cross_buf[...].T
    quarter = rows // 2
    place = 0
    for i in range(4):
        for j in range(i):
            tri_buf[place:place + quarter, :] = gram[i * quarter:(i + 1) * quarter, j * quarter:(j + 1) * quarter]
            place += quarter
    eighth = quarter // 2
    for i in range(4):
        low = i * quarter + eighth
        tri_buf[place:place + eighth, :] = gram[low:low + eighth, i * quarter:(i + 1) * quarter]
        place += eighth
    for i in (0, 2):
        first, second = i * quarter, (i + 1) * quarter
        tri_buf[place:place + eighth, :] = jnp.concatenate(
            [gram[first:first + eighth, first:first + eighth], gram[second:second + eighth, second:second + eighth]],
            axis=1,
        )
        place += eighth

    size = parts.shape[1]

    def piece(index):
        return pl.ds(pl.multiple_of(index * size, size), size)

    def part_copy(step):
        return pltpu.make_async_remote_copy(
            src_ref=tri_buf.at[piece(lax.rem(ring + step, count))],
            dst_ref=parts.at[ring],
            send_sem=sum_sem.at[0],
            recv_sem=sum_sem.at[1],
            device_id=ring_device(step),
            device_id_type=MESH,
        )

    def total_copy(step):
        return pltpu.make_async_remote_copy(
            src_ref=total.at[ring],
            dst_ref=total.at[ring],
            send_sem=sum_sem.at[2],
            recv_sem=sum_sem.at[3],
            device_id=ring_device(step),
            device_id_type=MESH,
        )

    far_first = sorted(range(1, count), key=lambda step: -min(step, count - step))
    for step in far_first:
        part_copy(step).start()
    early_copy(1).start()
    parts[ring] = tri_buf[piece(ring), :]
    pieces = parts.at[pl.ds(0, count - 1)]
    pltpu.make_async_copy(pieces, pieces, sum_sem.at[1]).wait()
    value = parts[0]
    for index in range(1, count):
        value = value + parts[index]
    total[ring] = value
    for step in far_first:
        total_copy(step).start()
    pltpu.make_async_copy(pieces, pieces, sum_sem.at[3]).wait()
    tri_ref[...] = total[...].reshape(tri_ref.shape)
    pltpu.make_async_copy(pieces, pieces, sum_sem.at[0]).wait()
    pltpu.make_async_copy(pieces, pieces, sum_sem.at[2]).wait()

    def write_early(index):
        return pltpu.make_async_copy(early_buf.at[index], early_hbm.at[index], early_sem.at[2, index])

    for index in range(EARLY):
        early_copy(index).wait_recv()
        write_early(index).start()
    for index in range(EARLY):
        early_copy(index).wait_send()
        write_early(index).wait()

    note_copy.wait()
    note_ref[...] = note_in[...]
    pltpu.make_async_copy(several, several, place_sem.at[0]).wait()

    def finish(index, carry):
        cross_copy(index).wait_send()
        write_other(index).wait()
        write_both(index).wait()
        return carry

    lax.fori_loop(0, half, finish, 0)
    for index in range(half - EARLY):
        write_own(index).wait()

    def sent(index, carry):
        pltpu.make_async_copy(
            out_buf.at[index, pl.ds(0, peers - 1)], out_buf.at[index, pl.ds(0, peers - 1)], out_sem.at[index]
        ).wait()
        return carry

    lax.fori_loop(0, CHUNKS, sent, 0)


def exchange(x, dest_ids, send_slot, peers, slots, row_count):
    rows, columns = x.shape
    width = columns // CHUNKS
    half = CHUNKS // 2
    count = 2 * row_count
    any_space = pl.BlockSpec(memory_space=pl.ANY)
    vmem = pl.BlockSpec(memory_space=pltpu.VMEM)
    smem = pl.BlockSpec(memory_space=pltpu.SMEM)
    return pl.pallas_call(
        functools.partial(exchange_kernel, peers, row_count, slots),
        out_shape=[
            jax.ShapeDtypeStruct((half - EARLY, rows, width), F32),
            jax.ShapeDtypeStruct((half, rows, width), F32),
            jax.ShapeDtypeStruct((half, 2 * rows, width), F32),
            jax.ShapeDtypeStruct((EARLY, rows, width), F32),
            jax.ShapeDtypeStruct((9 * rows // 2, rows // 2), F32),
            jax.ShapeDtypeStruct((2, 8, rows), F32),
        ],
        in_specs=[any_space, vmem, smem],
        out_specs=[any_space, any_space, any_space, any_space, vmem, vmem],
        scratch_shapes=[
            pltpu.VMEM((CHUNKS, rows, width), F32),
            pltpu.VMEM((CHUNKS, peers, slots, width), F32),
            pltpu.VMEM((CHUNKS, peers, slots, width), F32),
            pltpu.VMEM((half, 2 * rows, width), F32),
            pltpu.VMEM((half, rows, width), F32),
            pltpu.VMEM((EARLY, rows, width), F32),
            pltpu.VMEM((2 * rows, 2 * rows), F32),
            pltpu.VMEM((2 * rows, 2 * rows), F32),
            pltpu.VMEM((peers, slots, 128), F32),
            pltpu.VMEM((peers, slots, 128), F32),
            pltpu.VMEM((8, rows), F32),
            pltpu.VMEM((2, 8, rows), F32),
            pltpu.VMEM((9 * rows // 2, rows // 2), F32),
            pltpu.VMEM((count, 9 * rows // 2 // count, rows // 2), F32),
            pltpu.VMEM((count, 9 * rows // 2 // count, rows // 2), F32),
            pltpu.SemaphoreType.DMA((CHUNKS,)),
            pltpu.SemaphoreType.DMA((CHUNKS,)),
            pltpu.SemaphoreType.DMA((CHUNKS,)),
            pltpu.SemaphoreType.DMA((half,)),
            pltpu.SemaphoreType.DMA((half,)),
            pltpu.SemaphoreType.DMA((3 * half,)),
            pltpu.SemaphoreType.DMA((2,)),
            pltpu.SemaphoreType.DMA((2,)),
            pltpu.SemaphoreType.DMA((3, EARLY)),
            pltpu.SemaphoreType.DMA((4,)),
        ],
        compiler_params=pltpu.CompilerParams(
            collective_id=0, has_side_effects=True, vmem_limit_bytes=56 << 20
        ),
        cost_estimate=pl.CostEstimate(flops=10**10, bytes_accessed=10**8, transcendentals=0),
        name="exchange",
    )(x, dest_ids[None, :], send_slot)


def inverse_factors(blocks):
    size = BLOCK
    groups = size // 8
    sublane = lax.broadcasted_iota(jnp.int32, (8, 2 * size), 0)
    lane = lax.broadcasted_iota(jnp.int32, (8, 2 * size), 1)
    held = []
    for block in blocks:
        parts = []
        for g in range(groups):
            unit = (lane == sublane + (size + 8 * g)).astype(F32)
            left = jnp.concatenate([block[8 * g:8 * g + 8, :], jnp.zeros((8, size), F32)], axis=1)
            parts.append(left + unit)
        held.append(parts)
    pivots = 8
    wide = (8, 2 * size)
    for j in range(0, size, pivots):
        first, within = divmod(j, 8)
        for parts in held:
            top = [jnp.broadcast_to(parts[first][within + k:within + k + 1, :], wide) for k in range(pivots)]
            pivot = [
                [jnp.broadcast_to(top[k][:, j + m:j + m + 1], wide) for m in range(pivots)] for k in range(pivots)
            ]
            columns = [
                [jnp.broadcast_to(parts[g][:, j + k:j + k + 1], wide) for g in range(first, groups)]
                for k in range(pivots)
            ]
            scaled = []
            for k in range(pivots):
                inverse = 1.0 / pivot[k][k]
                for m in range(k + 1, pivots):
                    factor = pivot[k][m] * inverse
                    for n in range(m, pivots):
                        pivot[m][n] = pivot[m][n] - factor * pivot[k][n]
                    top[m] = top[m] - factor * top[k]
                    columns[m] = [c - factor * d for c, d in zip(columns[m], columns[k])]
                scaled.append(top[k] * inverse)
            for g in range(first, groups):
                value = parts[g]
                for k in range(pivots):
                    value = value - columns[k][g - first] * scaled[k]
                if g == first:
                    value = jnp.where(sublane >= within + pivots, value, parts[g])
                    for k in range(pivots):
                        value = jnp.where(sublane == within + k, top[k], value)
                parts[g] = value
    result = []
    for parts in held:
        rows = []
        for g in range(groups):
            pivot = jnp.sum(jnp.where(lane == sublane + 8 * g, parts[g], 0.0), axis=1, keepdims=True)
            rows.append(parts[g] * lax.rsqrt(pivot))
        result.append(jnp.concatenate(rows, axis=0)[:, size:])
    return result


def eliminate(work_refs, width):
    size = work_refs[0].shape[0]
    for start in range(0, size, BLOCK):
        stop = start + BLOCK
        inverses = inverse_factors([work[start:stop, start:stop] for work in work_refs])
        base = start - start % 128
        for work, inverse in zip(work_refs, inverses):
            top = dot_f32(inverse, work[start:stop, base:width])
            work[start:stop, base:width] = top
            if stop < size:
                below = top[:, stop - base:size - base]
                work[stop:size, base:width] = work[stop:size, base:width] - dot_f32(below, top, ((0,), (0,)))


def orthogonal_steps(grams, work_refs):
    size = grams[0].shape[0]
    row = lax.broadcasted_iota(jnp.int32, (size, size), 0)
    column = lax.broadcasted_iota(jnp.int32, (size, size), 1)
    for gram, work in zip(grams, work_refs):
        trace = jnp.sum(jnp.where(row == column, gram, 0.0))
        gram = gram * (size / trace)
        work[:, :size] = dot_f32(gram, gram)
    eliminate(work_refs, size)
    for work in work_refs:
        factor = jnp.where(row <= column, work[:, :size], 0.0)
        work[:, :size] = dot_f32(factor, factor, ((1,), (1,)))
        work[:, size:] = factor
    eliminate(work_refs, 2 * size)
    return [work[:, size:] for work in work_refs]


def rotation_kernel(tri_ref, note_ref, side_ref, high_ref, low_ref, gram_buf, work_a, work_b):
    quarter = tri_ref.shape[1]
    size = 2 * quarter
    place = 0
    for i in range(4):
        for j in range(i):
            block = tri_ref[place:place + quarter, :]
            gram_buf[i * quarter:(i + 1) * quarter, j * quarter:(j + 1) * quarter] = block
            gram_buf[j * quarter:(j + 1) * quarter, i * quarter:(i + 1) * quarter] = block.T
            place += quarter
    eighth = quarter // 2
    corners = place + 4 * eighth
    for i in range(4):
        lower = tri_ref[place:place + eighth, :]
        row = corners + i // 2 * eighth
        corner = tri_ref[row:row + eighth, i % 2 * eighth:(i % 2 + 1) * eighth]
        upper = jnp.concatenate([corner, lower[:, :eighth].T], axis=1)
        span = slice(i * quarter, (i + 1) * quarter)
        gram_buf[span, span] = jnp.concatenate([upper, lower], axis=0)
        place += eighth
    side = side_ref[0]
    position = jnp.concatenate([note_ref[0, :1], note_ref[1, :1]], axis=1)
    slot = lax.broadcasted_iota(jnp.int32, (2 * size, 2 * size), 0)
    slot = jnp.where(side == 0, slot, (slot + size) % (2 * size))
    place_of = (slot.astype(F32) == position).astype(BF16)
    own_slot = note_ref[side, 1:2, :1]
    partner_slot = note_ref[1 - side, 1:2, :1]
    half_way = select_rows(place_of, gram_buf[...])
    gram_buf[...] = select_rows(place_of, half_way.T)
    own = gram_buf[:size, :size]
    partner = gram_buf[size:, size:]
    between = gram_buf[:size, size:]
    own_turn, partner_turn = orthogonal_steps([own, partner], [work_a, work_b])
    own_part = jnp.where(own_slot == 0, own_turn[quarter:], own_turn[:quarter])
    partner_part = jnp.where(partner_slot == 0, partner_turn[:quarter], partner_turn[quarter:])
    nt = ((1,), (1,))
    upper = dot_f32(dot_f32(own_part, own), own_part, nt)
    lower = dot_f32(dot_f32(partner_part, partner), partner_part, nt)
    mixed = dot_f32(dot_f32(own_part, between), partner_part, nt)
    gram_buf[:quarter, :quarter] = upper
    gram_buf[quarter:size, quarter:size] = lower
    gram_buf[:quarter, quarter:size] = mixed
    gram_buf[quarter:size, :quarter] = mixed.T
    second = gram_buf[:size, :size]
    (last,) = orthogonal_steps([0.5 * (second + second.T)], [work_a])
    gram_buf[:size, :size] = dot_f32(last[:, :quarter], own_part)
    gram_buf[:size, size:] = dot_f32(last[:, quarter:], partner_part)
    high, middle, low = split3(gram_buf[:size, :])
    dot = functools.partial(jnp.dot, preferred_element_type=F32)
    weight = (dot(high, place_of) + dot(middle, place_of)) + dot(low, place_of)
    high = weight.astype(BF16)
    high_ref[...] = high
    low_ref[...] = (weight - high.astype(F32)).astype(BF16)


def rotations(tri, note, side):
    size = 2 * tri.shape[1]
    vmem = pl.BlockSpec(memory_space=pltpu.VMEM)
    smem = pl.BlockSpec(memory_space=pltpu.SMEM)
    return pl.pallas_call(
        rotation_kernel,
        out_shape=[jax.ShapeDtypeStruct((size, 2 * size), BF16)] * 2,
        in_specs=[vmem, vmem, smem],
        out_specs=[vmem, vmem],
        scratch_shapes=[
            pltpu.VMEM((2 * size, 2 * size), F32),
            pltpu.VMEM((size, 2 * size), F32),
            pltpu.VMEM((size, 2 * size), F32),
        ],
        compiler_params=pltpu.CompilerParams(vmem_limit_bytes=32 << 20),
        cost_estimate=pl.CostEstimate(flops=6 * 10**10, bytes_accessed=10**8, transcendentals=0),
        name="rotations",
    )(tri, note, side)


def product3(a_high, a_low, b):
    b_high = b.astype(BF16)
    b_low = (b - b_high.astype(F32)).astype(BF16)
    dot = functools.partial(jnp.dot, preferred_element_type=F32)
    return dot(a_high, b_high) + (dot(a_high, b_low) + dot(a_low, b_high))


def apply_both_kernel(side_ref, high_ref, low_ref, both_ref, out_ref):
    width = both_ref.shape[2]
    for k in range(TOGETHER):
        out_ref[:, k * width:(k + 1) * width] = product3(high_ref[...], low_ref[...], both_ref[k])


def apply_both(side, high, low, both, columns):
    chunks, rows, width = both.shape
    size = high.shape[0]
    steps = chunks // TOGETHER
    weight = pl.BlockSpec((size, rows), lambda i, s: (0, 0))
    return pl.pallas_call(
        apply_both_kernel,
        grid_spec=pltpu.PrefetchScalarGridSpec(
            num_scalar_prefetch=1,
            grid=(steps,),
            in_specs=[weight, weight, pl.BlockSpec((TOGETHER, rows, width), lambda i, s: (i, 0, 0))],
            out_specs=pl.BlockSpec((size, TOGETHER * width), lambda i, s: (0, s[0] * steps + i)),
        ),
        out_shape=jax.ShapeDtypeStruct((size, columns), F32),
        cost_estimate=pl.CostEstimate(flops=10**10, bytes_accessed=10**7, transcendentals=0),
        compiler_params=pltpu.CompilerParams(vmem_limit_bytes=32 << 20),
        name="apply_both",
    )(side, high, low, both)


def apply_rest_kernel(
    side_ref, high_ref, low_ref, mirror_high_ref, mirror_low_ref, own_ref, early_ref, mirror_ref, partial_ref, out_ref
):
    width = own_ref.shape[2]
    first = pl.program_id(0) == 0
    for k in range(TOGETHER):
        crossed = mirror_ref[k]
        if k < EARLY:
            crossed = jnp.where(first, early_ref[k], crossed)
        out_ref[:, k * width:(k + 1) * width] = product3(high_ref[...], low_ref[...], own_ref[k]) + product3(
            mirror_high_ref[...], mirror_low_ref[...], crossed
        )


def apply_rest(side, high, low, own, early, mirror, partial):
    chunks, rows, width = own.shape
    size = high.shape[0]
    steps = chunks // TOGETHER
    weight = pl.BlockSpec((size, rows), lambda i, s: (0, s[0]))
    mirror_weight = pl.BlockSpec((size, rows), lambda i, s: (0, 1 - s[0]))
    return pl.pallas_call(
        apply_rest_kernel,
        grid_spec=pltpu.PrefetchScalarGridSpec(
            num_scalar_prefetch=1,
            grid=(steps,),
            in_specs=[
                weight,
                weight,
                mirror_weight,
                mirror_weight,
                pl.BlockSpec((TOGETHER, rows, width), lambda i, s: (i, 0, 0)),
                pl.BlockSpec((EARLY, rows, width), lambda i, s: (0, 0, 0)),
                pl.BlockSpec((TOGETHER, rows, width), lambda i, s: (jnp.maximum(i - 1, 0), 0, 0)),
                pl.BlockSpec(memory_space=pl.ANY),
            ],
            out_specs=pl.BlockSpec((size, TOGETHER * width), lambda i, s: (0, (1 - s[0]) * steps + i)),
        ),
        out_shape=jax.ShapeDtypeStruct(partial.shape, F32),
        input_output_aliases={8: 0},
        cost_estimate=pl.CostEstimate(flops=10**10, bytes_accessed=10**7, transcendentals=0),
        compiler_params=pltpu.CompilerParams(vmem_limit_bytes=32 << 20),
        name="apply_rest",
    )(side, high, low, high, low, own, early, mirror, partial)


def body(row_count, greens_matrix, dest_ids, send_slot):
    rows, columns = greens_matrix.shape
    count = lax.axis_size("col")
    peers = count // 2
    cap = max(2, 2 * rows // count)
    slots = 2 * cap
    col = lax.axis_index("col")
    side = (col // peers).astype(jnp.int32)[None]
    own, other, both, early, tri, note = exchange(
        greens_matrix, dest_ids, send_slot, peers, slots, row_count
    )
    mirror = lax.ppermute(own, "col", [(i, i ^ peers) for i in range(count)])
    high, low = rotations(tri, note, side)
    partial = apply_both(side, high, low, both, columns)
    return apply_rest(side, high, low, other, early, mirror, partial)


def solution(mesh):
    return jax.shard_map(
        functools.partial(body, mesh.shape["row"]),
        mesh=mesh,
        in_specs=(P("col", "row"), P("col"), P("col")),
        out_specs=P("col", "row"),
        check_vma=False,
    )
```

```python
import functools

import jax
import jax.numpy as jnp
from jax import lax
from jax.experimental import pallas as pl
from jax.experimental.pallas import tpu as pltpu
from jax.sharding import PartitionSpec as P

CHUNKS = 16
EARLY = 2
TOGETHER = 2
LEAD = 3
BLOCK = 64
F32 = jnp.float32
BF16 = jnp.bfloat16
MESH = pl.DeviceIdType.MESH
HIGHEST = lax.Precision.HIGHEST


def split3(value):
    high = value.astype(BF16)
    rest = value - high.astype(F32)
    middle = rest.astype(BF16)
    low = (rest - middle.astype(F32)).astype(BF16)
    return high, middle, low


def select_rows(one_hot, value):
    high, middle, low = split3(value)
    dot = functools.partial(jnp.dot, one_hot, preferred_element_type=F32)
    return (dot(high) + dot(middle)) + dot(low)


def dot_f32(a, b, dims=((1,), (0,))):
    return lax.dot_general(a, b, (dims, ((), ())), precision=HIGHEST, preferred_element_type=F32)


def gram_update(rows):
    high, middle, low = split3(rows)
    nt = (((1,), (1,)), ((), ()))
    dot = functools.partial(lax.dot_general, dimension_numbers=nt, preferred_element_type=F32)
    cross = dot(middle, high) + dot(low, high)
    return dot(high, high) + dot(middle, middle) + cross, cross


def slot_tables(ids, col, peers, slots):
    rows = ids.shape[1]

    def log2(number):
        return number.bit_length() - 1

    def upright(values):
        return jnp.broadcast_to(values, (128, rows)).T[:, :1]

    target = lax.shift_right_logical(ids, log2(rows))
    peer = target & (peers - 1)
    row_place = (lax.shift_right_logical(target, log2(peers)) * rows + (ids & (rows - 1))).astype(F32)
    sender = upright(((col - ((target - col) & (peers - 1))) & (peers - 1)).astype(F32))
    peer = peer.astype(F32)
    earlier = lax.broadcasted_iota(jnp.int32, (rows, rows), 0) < lax.broadcasted_iota(jnp.int32, (rows, rows), 1)
    same = jnp.where(upright(peer) == peer, 1.0, 0.0)
    rank = jnp.sum(jnp.where(earlier, same, 0.0), axis=0, keepdims=True)
    slot = lax.broadcasted_iota(jnp.int32, (peers * slots, rows), 0).astype(F32)
    pack = (peer * slots + rank == slot).astype(BF16)
    incoming = lax.broadcasted_iota(jnp.int32, (rows, peers * slots), 1)
    origin = lax.shift_right_logical(incoming, log2(slots)).astype(F32)
    within = (incoming & (slots - 1))[:1].astype(F32)
    amount = jnp.sum(jnp.where(sender == origin, 1.0, 0.0), axis=0, keepdims=True)
    base = jnp.sum(jnp.where(sender < origin, 1.0, 0.0), axis=0, keepdims=True)
    wanted = jnp.where(within < amount, base + within, -1.0)
    place = lax.broadcasted_iota(jnp.int32, (rows, peers * slots), 0).astype(F32)
    return pack, (wanted == place).astype(BF16), row_place


def exchange_kernel(
    peers, row_count, slots, x_hbm, ids_ref, send_slot_ref,
    own_hbm, other_hbm, both_hbm, early_hbm, tri_ref, note_ref,
    x_buf, out_buf, in_buf, both_buf, other_buf, early_buf, gram_buf, cross_buf, place_out, place_in, note_out, note_in,
    tri_buf, parts, total,
    x_sem, out_sem, in_sem, z_out_sem, z_in_sem, write_sem, place_sem, note_sem, early_sem, sum_sem,
):
    col = lax.axis_index("col")
    side = col // peers
    me = col % peers
    mirror = lax.rem(col + peers, 2 * peers)
    half = CHUNKS // 2
    width = out_buf.shape[3]
    rows = other_buf.shape[1]

    def read_chunk(index):
        chunk = lax.rem((1 - side) * half + index, CHUNKS)
        piece = x_hbm.at[:, pl.ds(pl.multiple_of(chunk * width, width), width)]
        return pltpu.make_async_copy(piece, x_buf.at[index], x_sem.at[index])

    def start_read(index, carry):
        read_chunk(index).start()
        return carry

    lax.fori_loop(0, CHUNKS, start_read, 0)
    barrier = pltpu.get_barrier_semaphore()

    def greet(step, carry):
        peer = side * peers + lax.rem(me + step, peers)
        pl.semaphore_signal(barrier, inc=1, device_id={"col": peer}, device_id_type=MESH)
        return carry

    count = 2 * row_count
    ring = side * row_count + lax.axis_index("row")

    def ring_device(step):
        index = lax.rem(ring + step, count)
        return {"col": (index // row_count) * peers + me, "row": index % row_count}

    lax.fori_loop(1, peers, greet, 0)
    for step in range(1, count):
        pl.semaphore_signal(barrier, inc=1, device_id=ring_device(step), device_id_type=MESH)
    pl.semaphore_wait(barrier, peers - 1 + count - 1)

    pack, compact, row_place = slot_tables(ids_ref[...], col, peers, slots)

    def send_chunk(index, carry):
        read_chunk(index).wait()
        out_buf[index] = select_rows(pack, x_buf[index]).reshape(peers, slots, width)

        def send(step, inner):
            peer = lax.rem(me + step, peers)
            pltpu.make_async_remote_copy(
                src_ref=out_buf.at[index, peer],
                dst_ref=in_buf.at[index, me],
                send_sem=out_sem.at[index],
                recv_sem=in_sem.at[index],
                device_id={"col": side * peers + peer},
                device_id_type=MESH,
            ).start()
            return inner

        lax.fori_loop(1, peers, send, 0)
        in_buf[index, me] = out_buf[index, me]
        return carry

    def arrived(index):
        pltpu.make_async_copy(
            in_buf.at[index, pl.ds(0, peers - 1)], in_buf.at[index, pl.ds(0, peers - 1)], in_sem.at[index]
        ).wait()
        return select_rows(compact, in_buf[index].reshape(peers * slots, width))

    def cross_copy(index):
        return pltpu.make_async_remote_copy(
            src_ref=other_buf.at[index],
            dst_ref=both_buf.at[index, pl.ds(pl.multiple_of(side * rows, rows), rows)],
            send_sem=z_out_sem.at[index],
            recv_sem=z_in_sem.at[index],
            device_id={"col": mirror},
            device_id_type=MESH,
        )

    def write_other(index):
        return pltpu.make_async_copy(other_buf.at[index], other_hbm.at[index], write_sem.at[index])

    def write_own(index):
        source = both_buf.at[EARLY + index, pl.ds(pl.multiple_of(side * rows, rows), rows)]
        return pltpu.make_async_copy(source, own_hbm.at[index], write_sem.at[half + index])

    def write_both(index):
        return pltpu.make_async_copy(both_buf.at[index], both_hbm.at[index], write_sem.at[2 * half + index])

    def cross_chunk(index, carry):
        other_buf[index] = arrived(index)
        cross_copy(index).start()
        write_other(index).start()
        return carry

    def keep_chunk(index, carry):
        both_buf[index, pl.ds(pl.multiple_of(side * rows, rows), rows)] = arrived(half + index)
        return carry

    def send_and_cross(index, carry):
        cross_chunk(index, carry)
        return send_chunk(index + LEAD, carry)

    def send_and_keep(index, carry):
        send_chunk(half + index + LEAD, carry)
        return keep_chunk(index, carry)

    lax.fori_loop(0, LEAD, send_chunk, 0)
    lax.fori_loop(0, half, send_and_cross, 0)
    lax.fori_loop(0, half - LEAD, send_and_keep, 0)
    places = jnp.broadcast_to(row_place, (128, rows)).T
    place_out[...] = select_rows(pack, places).reshape(peers, slots, 128)

    def send_places(step, carry):
        peer = lax.rem(me + step, peers)
        pltpu.make_async_remote_copy(
            src_ref=place_out.at[peer],
            dst_ref=place_in.at[me],
            send_sem=place_sem.at[0],
            recv_sem=place_sem.at[1],
            device_id={"col": side * peers + peer},
            device_id_type=MESH,
        ).start()
        return carry

    lax.fori_loop(1, peers, send_places, 0)
    place_in[me] = place_out[me]

    lax.fori_loop(half - LEAD, half, keep_chunk, 0)
    for index in range(half - EARLY):
        write_own(index).start()

    several = place_in.at[pl.ds(0, peers - 1)]
    pltpu.make_async_copy(several, several, place_sem.at[1]).wait()
    listed = select_rows(compact, place_in[...].reshape(peers * slots, 128)).T[:8]
    first_row = lax.broadcasted_iota(jnp.int32, listed.shape, 0) == 0
    note_out[...] = jnp.where(first_row, listed, send_slot_ref[0].astype(F32))
    note_in[side] = note_out[...]
    note_copy = pltpu.make_async_remote_copy(
        src_ref=note_out,
        dst_ref=note_in.at[side],
        send_sem=note_sem.at[0],
        recv_sem=note_sem.at[1],
        device_id={"col": mirror},
        device_id_type=MESH,
    )
    note_copy.start()

    gram_buf[...] = jnp.zeros_like(gram_buf)
    cross_buf[...] = jnp.zeros_like(cross_buf)

    def early_copy(index):
        return pltpu.make_async_remote_copy(
            src_ref=both_buf.at[index, pl.ds(pl.multiple_of(side * rows, rows), rows)],
            dst_ref=early_buf.at[index],
            send_sem=early_sem.at[0, index],
            recv_sem=early_sem.at[1, index],
            device_id={"col": mirror},
            device_id_type=MESH,
        )

    def gram_chunk(index, carry):
        cross_copy(index).wait_recv()
        write_both(index).start()
        total, cross = gram_update(both_buf[index])
        gram_buf[...] += total
        cross_buf[...] += cross
        return carry

    lax.fori_loop(0, half - 1, gram_chunk, 0)
    early_copy(0).start()
    gram_chunk(half - 1, 0)
    gram = gram_buf[...] + cross_buf[...].T
    quarter = rows // 2
    place = 0
    for i in range(4):
        for j in range(i):
            tri_buf[place:place + quarter, :] = gram[i * quarter:(i + 1) * quarter, j * quarter:(j + 1) * quarter]
            place += quarter
    eighth = quarter // 2
    for i in range(4):
        low = i * quarter + eighth
        tri_buf[place:place + eighth, :] = gram[low:low + eighth, i * quarter:(i + 1) * quarter]
        place += eighth
    for i in (0, 2):
        first, second = i * quarter, (i + 1) * quarter
        tri_buf[place:place + eighth, :] = jnp.concatenate(
            [gram[first:first + eighth, first:first + eighth], gram[second:second + eighth, second:second + eighth]],
            axis=1,
        )
        place += eighth

    size = parts.shape[1]

    def piece(index):
        return pl.ds(pl.multiple_of(index * size, size), size)

    def part_copy(step):
        return pltpu.make_async_remote_copy(
            src_ref=tri_buf.at[piece(lax.rem(ring + step, count))],
            dst_ref=parts.at[ring],
            send_sem=sum_sem.at[0],
            recv_sem=sum_sem.at[1],
            device_id=ring_device(step),
            device_id_type=MESH,
        )

    def total_copy(step):
        return pltpu.make_async_remote_copy(
            src_ref=total.at[ring],
            dst_ref=total.at[ring],
            send_sem=sum_sem.at[2],
            recv_sem=sum_sem.at[3],
            device_id=ring_device(step),
            device_id_type=MESH,
        )

    far_first = sorted(range(1, count), key=lambda step: -min(step, count - step))
    for step in far_first:
        part_copy(step).start()
    early_copy(1).start()
    parts[ring] = tri_buf[piece(ring), :]
    pieces = parts.at[pl.ds(0, count - 1)]
    pltpu.make_async_copy(pieces, pieces, sum_sem.at[1]).wait()
    value = parts[0]
    for index in range(1, count):
        value = value + parts[index]
    total[ring] = value
    for step in far_first:
        total_copy(step).start()
    pltpu.make_async_copy(pieces, pieces, sum_sem.at[3]).wait()
    tri_ref[...] = total[...].reshape(tri_ref.shape)
    pltpu.make_async_copy(pieces, pieces, sum_sem.at[0]).wait()
    pltpu.make_async_copy(pieces, pieces, sum_sem.at[2]).wait()

    def write_early(index):
        return pltpu.make_async_copy(early_buf.at[index], early_hbm.at[index], early_sem.at[2, index])

    for index in range(EARLY):
        early_copy(index).wait_recv()
        write_early(index).start()
    for index in range(EARLY):
        early_copy(index).wait_send()
        write_early(index).wait()

    note_copy.wait()
    note_ref[...] = note_in[...]
    pltpu.make_async_copy(several, several, place_sem.at[0]).wait()

    def finish(index, carry):
        cross_copy(index).wait_send()
        write_other(index).wait()
        write_both(index).wait()
        return carry

    lax.fori_loop(0, half, finish, 0)
    for index in range(half - EARLY):
        write_own(index).wait()

    def sent(index, carry):
        pltpu.make_async_copy(
            out_buf.at[index, pl.ds(0, peers - 1)], out_buf.at[index, pl.ds(0, peers - 1)], out_sem.at[index]
        ).wait()
        return carry

    lax.fori_loop(0, CHUNKS, sent, 0)


def exchange(x, dest_ids, send_slot, peers, slots, row_count):
    rows, columns = x.shape
    width = columns // CHUNKS
    half = CHUNKS // 2
    count = 2 * row_count
    any_space = pl.BlockSpec(memory_space=pl.ANY)
    vmem = pl.BlockSpec(memory_space=pltpu.VMEM)
    smem = pl.BlockSpec(memory_space=pltpu.SMEM)
    return pl.pallas_call(
        functools.partial(exchange_kernel, peers, row_count, slots),
        out_shape=[
            jax.ShapeDtypeStruct((half - EARLY, rows, width), F32),
            jax.ShapeDtypeStruct((half, rows, width), F32),
            jax.ShapeDtypeStruct((half, 2 * rows, width), F32),
            jax.ShapeDtypeStruct((EARLY, rows, width), F32),
            jax.ShapeDtypeStruct((9 * rows // 2, rows // 2), F32),
            jax.ShapeDtypeStruct((2, 8, rows), F32),
        ],
        in_specs=[any_space, vmem, smem],
        out_specs=[any_space, any_space, any_space, any_space, vmem, vmem],
        scratch_shapes=[
            pltpu.VMEM((CHUNKS, rows, width), F32),
            pltpu.VMEM((CHUNKS, peers, slots, width), F32),
            pltpu.VMEM((CHUNKS, peers, slots, width), F32),
            pltpu.VMEM((half, 2 * rows, width), F32),
            pltpu.VMEM((half, rows, width), F32),
            pltpu.VMEM((EARLY, rows, width), F32),
            pltpu.VMEM((2 * rows, 2 * rows), F32),
            pltpu.VMEM((2 * rows, 2 * rows), F32),
            pltpu.VMEM((peers, slots, 128), F32),
            pltpu.VMEM((peers, slots, 128), F32),
            pltpu.VMEM((8, rows), F32),
            pltpu.VMEM((2, 8, rows), F32),
            pltpu.VMEM((9 * rows // 2, rows // 2), F32),
            pltpu.VMEM((count, 9 * rows // 2 // count, rows // 2), F32),
            pltpu.VMEM((count, 9 * rows // 2 // count, rows // 2), F32),
            pltpu.SemaphoreType.DMA((CHUNKS,)),
            pltpu.SemaphoreType.DMA((CHUNKS,)),
            pltpu.SemaphoreType.DMA((CHUNKS,)),
            pltpu.SemaphoreType.DMA((half,)),
            pltpu.SemaphoreType.DMA((half,)),
            pltpu.SemaphoreType.DMA((3 * half,)),
            pltpu.SemaphoreType.DMA((2,)),
            pltpu.SemaphoreType.DMA((2,)),
            pltpu.SemaphoreType.DMA((3, EARLY)),
            pltpu.SemaphoreType.DMA((4,)),
        ],
        compiler_params=pltpu.CompilerParams(
            collective_id=0, has_side_effects=True, vmem_limit_bytes=56 << 20
        ),
        cost_estimate=pl.CostEstimate(flops=10**10, bytes_accessed=10**8, transcendentals=0),
        name="exchange",
    )(x, dest_ids[None, :], send_slot)


def inverse_factors(blocks):
    size = BLOCK
    groups = size // 8
    sublane = lax.broadcasted_iota(jnp.int32, (8, 2 * size), 0)
    lane = lax.broadcasted_iota(jnp.int32, (8, 2 * size), 1)
    held = []
    for block in blocks:
        parts = []
        for g in range(groups):
            unit = (lane == sublane + (size + 8 * g)).astype(F32)
            left = jnp.concatenate([block[8 * g:8 * g + 8, :], jnp.zeros((8, size), F32)], axis=1)
            parts.append(left + unit)
        held.append(parts)
    pivots = 8
    wide = (8, 2 * size)
    for j in range(0, size, pivots):
        first, within = divmod(j, 8)
        for parts in held:
            top = [jnp.broadcast_to(parts[first][within + k:within + k + 1, :], wide) for k in range(pivots)]
            pivot = [
                [jnp.broadcast_to(top[k][:, j + m:j + m + 1], wide) for m in range(pivots)] for k in range(pivots)
            ]
            columns = [
                [jnp.broadcast_to(parts[g][:, j + k:j + k + 1], wide) for g in range(first, groups)]
                for k in range(pivots)
            ]
            scaled = []
            for k in range(pivots):
                inverse = 1.0 / pivot[k][k]
                for m in range(k + 1, pivots):
                    factor = pivot[k][m] * inverse
                    for n in range(m, pivots):
                        pivot[m][n] = pivot[m][n] - factor * pivot[k][n]
                    top[m] = top[m] - factor * top[k]
                    columns[m] = [c - factor * d for c, d in zip(columns[m], columns[k])]
                scaled.append(top[k] * inverse)
            for g in range(first, groups):
                value = parts[g]
                for k in range(pivots):
                    value = value - columns[k][g - first] * scaled[k]
                if g == first:
                    value = jnp.where(sublane >= within + pivots, value, parts[g])
                    for k in range(pivots):
                        value = jnp.where(sublane == within + k, top[k], value)
                parts[g] = value
    result = []
    for parts in held:
        rows = []
        for g in range(groups):
            pivot = jnp.sum(jnp.where(lane == sublane + 8 * g, parts[g], 0.0), axis=1, keepdims=True)
            rows.append(parts[g] * lax.rsqrt(pivot))
        result.append(jnp.concatenate(rows, axis=0)[:, size:])
    return result


def eliminate(work_refs, width):
    size = work_refs[0].shape[0]
    for start in range(0, size, BLOCK):
        stop = start + BLOCK
        inverses = inverse_factors([work[start:stop, start:stop] for work in work_refs])
        base = start - start % 128
        for work, inverse in zip(work_refs, inverses):
            top = dot_f32(inverse, work[start:stop, base:width])
            work[start:stop, base:width] = top
            if stop < size:
                below = top[:, stop - base:size - base]
                work[stop:size, base:width] = work[stop:size, base:width] - dot_f32(below, top, ((0,), (0,)))


def orthogonal_steps(grams, work_refs):
    size = grams[0].shape[0]
    row = lax.broadcasted_iota(jnp.int32, (size, size), 0)
    column = lax.broadcasted_iota(jnp.int32, (size, size), 1)
    for gram, work in zip(grams, work_refs):
        trace = jnp.sum(jnp.where(row == column, gram, 0.0))
        gram = gram * (size / trace)
        work[:, :size] = dot_f32(gram, gram)
    eliminate(work_refs, size)
    for work in work_refs:
        factor = jnp.where(row <= column, work[:, :size], 0.0)
        work[:, :size] = dot_f32(factor, factor, ((1,), (1,)))
        work[:, size:] = factor
    eliminate(work_refs, 2 * size)
    return [work[:, size:] for work in work_refs]


def rotation_kernel(tri_ref, note_ref, side_ref, high_ref, low_ref, gram_buf, work_a, work_b):
    quarter = tri_ref.shape[1]
    size = 2 * quarter
    place = 0
    for i in range(4):
        for j in range(i):
            block = tri_ref[place:place + quarter, :]
            gram_buf[i * quarter:(i + 1) * quarter, j * quarter:(j + 1) * quarter] = block
            gram_buf[j * quarter:(j + 1) * quarter, i * quarter:(i + 1) * quarter] = block.T
            place += quarter
    eighth = quarter // 2
    corners = place + 4 * eighth
    for i in range(4):
        lower = tri_ref[place:place + eighth, :]
        row = corners + i // 2 * eighth
        corner = tri_ref[row:row + eighth, i % 2 * eighth:(i % 2 + 1) * eighth]
        upper = jnp.concatenate([corner, lower[:, :eighth].T], axis=1)
        span = slice(i * quarter, (i + 1) * quarter)
        gram_buf[span, span] = jnp.concatenate([upper, lower], axis=0)
        place += eighth
    side = side_ref[0]
    position = jnp.concatenate([note_ref[0, :1], note_ref[1, :1]], axis=1)
    slot = lax.broadcasted_iota(jnp.int32, (2 * size, 2 * size), 0)
    slot = jnp.where(side == 0, slot, (slot + size) % (2 * size))
    place_of = (slot.astype(F32) == position).astype(BF16)
    own_slot = note_ref[side, 1:2, :1]
    partner_slot = note_ref[1 - side, 1:2, :1]
    half_way = select_rows(place_of, gram_buf[...])
    gram_buf[...] = select_rows(place_of, half_way.T)
    own = gram_buf[:size, :size]
    partner = gram_buf[size:, size:]
    between = gram_buf[:size, size:]
    own_turn, partner_turn = orthogonal_steps([own, partner], [work_a, work_b])
    own_part = jnp.where(own_slot == 0, own_turn[quarter:], own_turn[:quarter])
    partner_part = jnp.where(partner_slot == 0, partner_turn[:quarter], partner_turn[quarter:])
    nt = ((1,), (1,))
    upper = dot_f32(dot_f32(own_part, own), own_part, nt)
    lower = dot_f32(dot_f32(partner_part, partner), partner_part, nt)
    mixed = dot_f32(dot_f32(own_part, between), partner_part, nt)
    gram_buf[:quarter, :quarter] = upper
    gram_buf[quarter:size, quarter:size] = lower
    gram_buf[:quarter, quarter:size] = mixed
    gram_buf[quarter:size, :quarter] = mixed.T
    second = gram_buf[:size, :size]
    (last,) = orthogonal_steps([0.5 * (second + second.T)], [work_a])
    gram_buf[:size, :size] = dot_f32(last[:, :quarter], own_part)
    gram_buf[:size, size:] = dot_f32(last[:, quarter:], partner_part)
    high, middle, low = split3(gram_buf[:size, :])
    dot = functools.partial(jnp.dot, preferred_element_type=F32)
    weight = (dot(high, place_of) + dot(middle, place_of)) + dot(low, place_of)
    high = weight.astype(BF16)
    high_ref[...] = high
    low_ref[...] = (weight - high.astype(F32)).astype(BF16)


def rotations(tri, note, side):
    size = 2 * tri.shape[1]
    vmem = pl.BlockSpec(memory_space=pltpu.VMEM)
    smem = pl.BlockSpec(memory_space=pltpu.SMEM)
    return pl.pallas_call(
        rotation_kernel,
        out_shape=[jax.ShapeDtypeStruct((size, 2 * size), BF16)] * 2,
        in_specs=[vmem, vmem, smem],
        out_specs=[vmem, vmem],
        scratch_shapes=[
            pltpu.VMEM((2 * size, 2 * size), F32),
            pltpu.VMEM((size, 2 * size), F32),
            pltpu.VMEM((size, 2 * size), F32),
        ],
        compiler_params=pltpu.CompilerParams(vmem_limit_bytes=32 << 20),
        cost_estimate=pl.CostEstimate(flops=6 * 10**10, bytes_accessed=10**8, transcendentals=0),
        name="rotations",
    )(tri, note, side)


def product3(a_high, a_low, b):
    b_high = b.astype(BF16)
    b_low = (b - b_high.astype(F32)).astype(BF16)
    dot = functools.partial(jnp.dot, preferred_element_type=F32)
    return dot(a_high, b_high) + (dot(a_high, b_low) + dot(a_low, b_high))


def apply_both_kernel(side_ref, high_ref, low_ref, both_ref, out_ref):
    width = both_ref.shape[2]
    for k in range(TOGETHER):
        out_ref[:, k * width:(k + 1) * width] = product3(high_ref[...], low_ref[...], both_ref[k])


def apply_both(side, high, low, both, columns):
    chunks, rows, width = both.shape
    size = high.shape[0]
    steps = chunks // TOGETHER
    weight = pl.BlockSpec((size, rows), lambda i, s: (0, 0))
    return pl.pallas_call(
        apply_both_kernel,
        grid_spec=pltpu.PrefetchScalarGridSpec(
            num_scalar_prefetch=1,
            grid=(steps,),
            in_specs=[weight, weight, pl.BlockSpec((TOGETHER, rows, width), lambda i, s: (i, 0, 0))],
            out_specs=pl.BlockSpec((size, TOGETHER * width), lambda i, s: (0, s[0] * steps + i)),
        ),
        out_shape=jax.ShapeDtypeStruct((size, columns), F32),
        cost_estimate=pl.CostEstimate(flops=10**10, bytes_accessed=10**7, transcendentals=0),
        compiler_params=pltpu.CompilerParams(vmem_limit_bytes=32 << 20),
        name="apply_both",
    )(side, high, low, both)


def apply_rest_kernel(
    side_ref, high_ref, low_ref, mirror_high_ref, mirror_low_ref, own_ref, early_ref, mirror_ref, partial_ref, out_ref
):
    width = own_ref.shape[2]
    first = pl.program_id(0) == 0
    for k in range(TOGETHER):
        crossed = mirror_ref[k]
        if k < EARLY:
            crossed = jnp.where(first, early_ref[k], crossed)
        out_ref[:, k * width:(k + 1) * width] = product3(high_ref[...], low_ref[...], own_ref[k]) + product3(
            mirror_high_ref[...], mirror_low_ref[...], crossed
        )


def apply_rest(side, high, low, own, early, mirror, partial):
    chunks, rows, width = own.shape
    size = high.shape[0]
    steps = chunks // TOGETHER
    weight = pl.BlockSpec((size, rows), lambda i, s: (0, s[0]))
    mirror_weight = pl.BlockSpec((size, rows), lambda i, s: (0, 1 - s[0]))
    return pl.pallas_call(
        apply_rest_kernel,
        grid_spec=pltpu.PrefetchScalarGridSpec(
            num_scalar_prefetch=1,
            grid=(steps,),
            in_specs=[
                weight,
                weight,
                mirror_weight,
                mirror_weight,
                pl.BlockSpec((TOGETHER, rows, width), lambda i, s: (i, 0, 0)),
                pl.BlockSpec((EARLY, rows, width), lambda i, s: (0, 0, 0)),
                pl.BlockSpec((TOGETHER, rows, width), lambda i, s: (jnp.maximum(i - 1, 0), 0, 0)),
                pl.BlockSpec(memory_space=pl.ANY),
            ],
            out_specs=pl.BlockSpec((size, TOGETHER * width), lambda i, s: (0, (1 - s[0]) * steps + i)),
        ),
        out_shape=jax.ShapeDtypeStruct(partial.shape, F32),
        input_output_aliases={8: 0},
        cost_estimate=pl.CostEstimate(flops=10**10, bytes_accessed=10**7, transcendentals=0),
        compiler_params=pltpu.CompilerParams(vmem_limit_bytes=32 << 20),
        name="apply_rest",
    )(side, high, low, high, low, own, early, mirror, partial)


def body(row_count, greens_matrix, dest_ids, send_slot):
    rows, columns = greens_matrix.shape
    count = lax.axis_size("col")
    peers = count // 2
    cap = max(2, 2 * rows // count)
    slots = 2 * cap
    col = lax.axis_index("col")
    side = (col // peers).astype(jnp.int32)[None]
    own, other, both, early, tri, note = exchange(
        greens_matrix, dest_ids, send_slot, peers, slots, row_count
    )
    mirror = lax.ppermute(own, "col", [(i, i ^ peers) for i in range(count)])
    high, low = rotations(tri, note, side)
    partial = apply_both(side, high, low, both, columns)
    return apply_rest(side, high, low, other, early, mirror, partial)


def solution(mesh):
    return jax.shard_map(
        functools.partial(body, mesh.shape["row"]),
        mesh=mesh,
        in_specs=(P("col", "row"), P("col"), P("col")),
        out_specs=P("col", "row"),
        check_vma=False,
    )
```
